512 devices in a mesh: dp: 64 (over z, y_lo, core), tensor: 8 (over x, y_hi).
Axes of the slice: x: 4, y: 4 (y_hi: 2, y_lo: 2; y = y_hi * 2 + y_lo), z: 16, core: 2. Of those that a mesh axis runs over, the one named last changes fastest.
Arguments:
- inputs: bfloat16 [16384, 4096], P('dp', 'tensor'), may hold values from -6 to 6
- cotangent: bfloat16 [16384, 4096], P('dp', 'tensor'), may hold values from -6 to 6
- gate_pre: bfloat16 [16384, 11008], P('dp', 'tensor'), may hold values from -6 to 6
- up_pre: bfloat16 [16384, 11008], P('dp', 'tensor'), may hold values from -6 to 6
- down_weight: bfloat16 [11008, 4096], P('tensor', 'dp'), may hold values from -0.0546875 to 0.0546875
- proj_in_x: bfloat16 [4096, 128], P('tensor'), may hold values from -0.09375 to 0.09375
- proj_in_h: bfloat16 [11008, 64], P('tensor'), may hold values from -0.0546875 to 0.0546875
- proj_out_ff: bfloat16 [11008, 128], P('tensor'), may hold values from -0.0546875 to 0.0546875
- proj_out_d: bfloat16 [4096, 64], P('tensor'), may hold values from -0.09375 to 0.09375
- queries: bfloat16 [8192, 12288], P('dp', 'tensor'), may hold values from -0.0546875 to 0.0546875
- lengths: int32 [8], replicated, may hold values from 512 to 2048
Outputs:
- scores: float32 [8, 8192], P(None, 'dp')
The draws below stay inside these ranges and needn't reach their ends.
All inputs are finite; a program needn't handle non-finite values.
Results may differ from the reference program's by a relative error of at most 0.0029.
Values may be sent and summed in bfloat16 or wider, within the bound.
No kernel may reach another device: no remote copies, remote signals or barrier semaphores. Data moves between devices by JAX's collectives and lax.ppermute only.
A program may use at most 64 MiB of HBM per device.

```python
import math
import jax
import jax.numpy as jnp
from jax import lax

D = 4096
FF = 11008
R = 64
LEN = 2048
SESSIONS = 8
TOKENS = 16384
QUERIES = 8192


def with_ends(array, own_key, least, top_value):
    longest = array.shape.index(max(array.shape))
    spots = []
    for shift in (0, 1):
        where = [jax.random.randint(jax.random.fold_in(own_key, axis), (), 0, length) for axis, length in enumerate(array.shape)]
        where[longest] = (where[longest] + shift) % array.shape[longest]
        spots.append(tuple(where))
    return array.at[spots[0]].set(least).at[spots[1]].set(top_value)


def block_levels(rng, dims, pieces, smallest, largest):
    def one(position, shards_of):
        steps = jax.random.uniform(jax.random.fold_in(jax.random.fold_in(rng, 6), position), (shards_of,), jnp.float32, smallest / len(pieces), largest / len(pieces))
        return jnp.repeat(jnp.exp(steps), dims[position] // shards_of).reshape((-1,) + (1,) * (len(dims) - position - 1))

    loudness = one(*pieces[0])
    for cut in pieces[1:]:
        loudness = loudness * one(*cut)
    return loudness


def normal_values(stream_key, dims, width, reach, split=(), dtype=jnp.bfloat16):
    entries = jax.random.normal(stream_key, dims, jnp.float32) * width
    if len(split) > 0:
        entries = block_levels(stream_key, dims, split, -0.22, 0.18) * entries
    return jnp.clip(entries, min=-reach, max=reach).astype(dtype)


def setup_inputs(seed: int = 0) -> dict:
    seeds = jax.random.split(jax.random.key(seed), 12)
    return {
        "inputs": normal_values(seeds[0], (TOKENS, D), 1.0, 6.0, ((0, 64), (1, 8))),
        "cotangent": normal_values(seeds[1], (TOKENS, D), 1.0, 6.0, ((0, 64), (1, 8))),
        "gate_pre": normal_values(seeds[2], (TOKENS, FF), 1.0, 6.0, ((0, 64), (1, 8))),
        "up_pre": normal_values(seeds[3], (TOKENS, FF), 1.0, 6.0, ((0, 64), (1, 8))),
        "down_weight": normal_values(seeds[4], (FF, D), FF ** -0.5, 0.0546875, ((0, 8), (1, 64))),
        "proj_in_x": normal_values(seeds[5], (D, 2 * R), D ** -0.5, 0.09375, ((0, 8),)),
        "proj_in_h": normal_values(seeds[6], (FF, R), FF ** -0.5, 0.0546875, ((0, 8),)),
        "proj_out_ff": normal_values(seeds[7], (FF, 2 * R), FF ** -0.5, 0.0546875, ((0, 8),)),
        "proj_out_d": normal_values(seeds[8], (D, R), D ** -0.5, 0.09375, ((0, 8),)),
        "queries": normal_values(seeds[9], (QUERIES, 3 * R * R), (3 * R * R) ** -0.5, 0.0546875, ((0, 64), (1, 8))),
        "lengths": with_ends(jax.random.randint(seeds[10], (SESSIONS,), LEN // 4, LEN + 1), jax.random.fold_in(seeds[10], 1), LEN // 4, LEN).astype(jnp.int32),
    }


def reference(inputs, cotangent, gate_pre, up_pre, down_weight, proj_in_x, proj_in_h, proj_out_ff, proj_out_d, queries, lengths):

    def per_session(packed):
        ses_inputs, ses_cot, ses_gate, ses_up, ses_length = packed
        live_mask = (jnp.arange(LEN) < ses_length).astype(jnp.float32)[:, None]
        gate_float = ses_gate.astype(jnp.float32)
        up_float = ses_up.astype(jnp.float32)
        gate_sigmoid = jax.nn.sigmoid(gate_float)
        gate_silu = gate_float * gate_sigmoid
        hidden = (gate_silu * up_float).astype(jnp.bfloat16)
        grad_hidden = jnp.dot(ses_cot, down_weight.T, preferred_element_type=jnp.float32)
        grad_gate = (grad_hidden * up_float * gate_sigmoid * (1.0 + gate_float * (1.0 - gate_sigmoid))).astype(jnp.bfloat16)
        grad_up = (grad_hidden * gate_silu).astype(jnp.bfloat16)
        proj_x = jnp.dot(ses_inputs, proj_in_x, preferred_element_type=jnp.float32)
        proj_h = jnp.dot(hidden, proj_in_h, preferred_element_type=jnp.float32)
        proj_gate = jnp.dot(grad_gate, proj_out_ff[:, :R], preferred_element_type=jnp.float32)
        proj_up = jnp.dot(grad_up, proj_out_ff[:, R:], preferred_element_type=jnp.float32)
        proj_d = jnp.dot(ses_cot, proj_out_d, preferred_element_type=jnp.float32)
        inputs_side = jnp.stack([proj_x[:, :R], proj_x[:, R:], proj_h])
        outputs_side = jnp.stack([proj_gate, proj_up, proj_d]) * live_mask[None]
        blocks = jnp.einsum('ltr,lts->lrs', inputs_side, outputs_side, precision=lax.Precision.HIGHEST)
        return blocks.reshape(-1)
    session_grads = lax.map(per_session, (inputs.reshape(SESSIONS, LEN, D), cotangent.reshape(SESSIONS, LEN, D), gate_pre.reshape(SESSIONS, LEN, FF), up_pre.reshape(SESSIONS, LEN, FF), lengths))
    score_scale = 1.0 / math.sqrt(LEN)
    return jnp.dot(session_grads, queries.astype(jnp.float32).T, precision=lax.Precision.HIGHEST) * score_scale
```

```python
import math

import jax
import jax.numpy as jnp
from jax import lax
from jax.sharding import Mesh
from jax.sharding import PartitionSpec as P

LEN = 2048
DP = ("zh", "zl", "yl", "c")
TENSOR = ("x", "yh")
SWAP = [(0, 1), (1, 0)]
HIGHEST = lax.Precision.HIGHEST


def dot(a, b):
    return jnp.dot(a, b, preferred_element_type=jnp.float32)


def split_dot(a, b):
    high = a.astype(jnp.bfloat16)
    low = (a - high.astype(jnp.float32)).astype(jnp.bfloat16)
    return dot(high, b) + dot(low, b)


def give_all(block, axes):
    n = lax.axis_size(axes)
    return lax.all_to_all(jnp.broadcast_to(block[None], (n,) + block.shape), axes, 0, 0)


def on_device(
    inputs,
    cotangent,
    gate_pre,
    up_pre,
    down_weight,
    proj_in_x,
    proj_in_h,
    proj_out_ff,
    proj_out_d,
    queries,
    lengths,
):
    rows, width = cotangent.shape
    hid = gate_pre.shape[1]
    rank = proj_in_h.shape[1]
    own_yl = lax.axis_index("yl")
    tensor_size = lax.axis_size(TENSOR)

    weight = lax.all_gather(down_weight.T, ("zh", "zl", "c"), axis=0, tiled=True)

    halves = cotangent.reshape(rows, -1, 2, 2 * down_weight.shape[1])
    first, second = (halves[:, :, i].reshape(rows, width // 2) for i in (0, 1))
    mine = jnp.where(own_yl == 0, first, second)
    theirs = jnp.where(own_yl == 0, second, first)
    both_cot = jnp.concatenate([mine, lax.ppermute(theirs, "yl", SWAP)], axis=0)
    partner_pre = lax.ppermute(jnp.concatenate([gate_pre, up_pre], axis=0), "yl", SWAP)
    full_cot = give_all(both_cot, TENSOR)

    gate_float = jnp.concatenate([gate_pre, partner_pre[:rows]], axis=0).astype(jnp.float32)
    up_float = jnp.concatenate([up_pre, partner_pre[rows:]], axis=0).astype(jnp.float32)
    sig = jax.nn.sigmoid(gate_float)
    silu = gate_float * sig
    gate_slope = up_float * sig * (1.0 + gate_float * (1.0 - sig))
    own_gate = gate_pre.astype(jnp.float32)
    hidden = (own_gate * jax.nn.sigmoid(own_gate) * up_pre.astype(jnp.float32)).astype(jnp.bfloat16)

    parts = jnp.concatenate(
        [dot(inputs, proj_in_x), dot(hidden, proj_in_h), dot(cotangent, proj_out_d)], axis=1
    )
    some = rows // tensor_size
    sums = lax.all_to_all(parts.reshape(tensor_size, some, 4 * rank), TENSOR, 0, 0).sum(axis=0)
    first_event = lax.axis_index(DP) * rows + lax.axis_index(TENSOR) * some
    positions = first_event % LEN + jnp.arange(some, dtype=jnp.int32)
    live = (positions < lengths[first_event // LEN]).astype(jnp.float32)[:, None]
    sums_x, sums_h, sums_d = sums[:, : 2 * rank] * live, sums[:, 2 * rank : 3 * rank], sums[:, 3 * rank :]
    block_d = jnp.einsum("tr,ts->rs", sums_h, sums_d * live, precision=HIGHEST)
    proj_x = give_all(sums_x, ("yl",) + TENSOR).reshape(2, rows, 2 * rank)
    proj_x = jnp.where(own_yl == 0, proj_x, proj_x[::-1]).reshape(2 * rows, 2 * rank)

    grad_hidden = lax.dot_general(
        full_cot,
        weight.reshape(tensor_size, width // 2, hid),
        (((0, 2), (0, 1)), ((), ())),
        preferred_element_type=jnp.float32,
    )
    proj_gate = split_dot(grad_hidden * gate_slope, proj_out_ff[:, :rank])
    proj_up = split_dot(grad_hidden * silu, proj_out_ff[:, rank:])
    block_g = jnp.einsum("tr,ts->rs", proj_x[:, :rank], proj_gate, precision=HIGHEST)
    block_u = jnp.einsum("tr,ts->rs", proj_x[:, rank:], proj_up, precision=HIGHEST)

    blocks = jnp.concatenate([block_g, block_u, block_d], axis=0)
    group = ("zl", "yl", "c")
    members = tensor_size * lax.axis_size(group)
    piece = lax.all_to_all(blocks.reshape(members, -1), TENSOR + group, 0, 0).sum(axis=0)
    pieces = give_all(piece, ("zh",))
    session_grads = give_all(pieces, group).transpose(1, 0, 2).reshape(pieces.shape[0], -1)
    partial_scores = lax.dot_general(
        session_grads,
        queries.astype(jnp.float32),
        (((1,), (1,)), ((), ())),
        precision=HIGHEST,
    ) * (1.0 / math.sqrt(LEN))
    return give_all(partial_scores, TENSOR).sum(axis=0)


def solution(mesh):
    fine = Mesh(mesh.devices.reshape(8, 2, 2, 2, 4, 2), DP + TENSOR)
    return jax.shard_map(
        on_device,
        mesh=fine,
        in_specs=(
            P(DP, TENSOR),
            P(DP, TENSOR),
            P(DP, TENSOR),
            P(DP, TENSOR),
            P(TENSOR, DP),
            P(TENSOR, None),
            P(TENSOR, None),
            P(TENSOR, None),
            P(TENSOR, None),
            P(DP, TENSOR),
            P(),
        ),
        out_specs=P(None, DP),
        check_vma=False,
    )
```

```python
import functools
import math

import jax
import jax.numpy as jnp
from jax import lax
from jax.experimental import pallas as pl
from jax.experimental.pallas import tpu as pltpu
from jax.sharding import Mesh
from jax.sharding import PartitionSpec as P

LEN = 2048
TILE = 384
DP = ("zh", "zl", "yl", "c")
TENSOR = ("x", "yh")
QUERY_GROUP = ("yl", "c")
SHARE = TENSOR + QUERY_GROUP
SWAP = [(0, 1), (1, 0)]
HIGHEST = lax.Precision.HIGHEST
VMEM = pl.BlockSpec(memory_space=pltpu.VMEM)


def dot(a, b):
    return jnp.dot(a, b, preferred_element_type=jnp.float32)


def split_dot(a, b):
    high = a.astype(jnp.bfloat16)
    low = (a - high.astype(jnp.float32)).astype(jnp.bfloat16)
    return dot(high, b) + dot(low, b)


def gradient_kernel(cot_ref, weight_ref, slope_ref, silu_ref, proj_ref, x_ref, down_ref, out_ref, held, part, rows_ref, sems):
    pieces, events, depth = cot_ref.shape
    hid = slope_ref.shape[1]
    rank = down_ref.shape[0]
    chunks = sems.shape[0]
    span = pieces * depth // chunks
    copies = [
        pltpu.make_async_copy(weight_ref.at[pl.ds(i * span, span)], held.at[pl.ds(i * span, span)], sems.at[i])
        for i in range(chunks)
    ]
    for copy in copies:
        copy.start()
    starts = list(range(0, hid, TILE))

    def product(tile, which):
        total = None
        for i in which:
            term = dot(cot_ref[i], held[pl.ds(i * depth, depth), tile])
            total = term if total is None else total + term
        return total

    early = pieces // 2
    for copy in copies[: chunks // 2]:
        copy.wait()
    for start in starts:
        tile = slice(start, min(start + TILE, hid))
        part[:, tile] = product(tile, range(early))
    for copy in copies[chunks // 2 :]:
        copy.wait()
    gate_sum = up_sum = None
    for start in starts:
        tile = slice(start, min(start + TILE, hid))
        grad = part[:, tile] + product(tile, range(early, pieces))
        proj = proj_ref[tile, :]
        gate_term = split_dot(grad * slope_ref[:, tile], proj)
        up_term = split_dot(grad * silu_ref[:, tile], proj)
        gate_sum = gate_term if gate_sum is None else gate_sum + gate_term
        up_sum = up_term if up_sum is None else up_sum + up_term
    lane = lax.broadcasted_iota(jnp.int32, gate_sum.shape, 1)
    both = jnp.where(lane < rank, gate_sum, up_sum)
    square = jnp.dot(x_ref[...], both, precision=HIGHEST, preferred_element_type=jnp.float32)
    rows_ref[:rank, :rank] = square[:rank, :rank]
    rows_ref[rank : 2 * rank, :rank] = square[rank:, rank:]
    rows_ref[2 * rank :, :rank] = down_ref[...]
    rows_ref[:, rank:] = jnp.zeros_like(rows_ref[:, rank:])
    members = out_ref.shape[0]
    each = rows_ref.shape[0] // members
    for i in range(each):
        row = rows_ref[pl.ds(i, members, stride=each), :]
        out_ref[:, :, i * rank : (i + 1) * rank] = row[:, None, :rank]


def gradient_blocks(cot, weight, slope, silu, proj, proj_x, block_d, members):
    rank = block_d.shape[0]
    return pl.pallas_call(
        gradient_kernel,
        out_shape=jax.ShapeDtypeStruct((members, 1, 3 * rank * rank // members), jnp.float32),
        in_specs=[VMEM, pl.BlockSpec(memory_space=pltpu.HBM)] + [VMEM] * 5,
        out_specs=VMEM,
        scratch_shapes=[
            pltpu.VMEM(weight.shape, jnp.bfloat16),
            pltpu.VMEM(slope.shape, jnp.float32),
            pltpu.VMEM((3 * rank, 2 * rank), jnp.float32),
            pltpu.SemaphoreType.DMA((4,)),
        ],
        compiler_params=pltpu.CompilerParams(vmem_limit_bytes=40 * 2**20),
        cost_estimate=pl.CostEstimate(
            flops=2 * slope.shape[0] * weight.shape[0] * weight.shape[1],
            bytes_accessed=weight.size * 2,
            transcendentals=0,
        ),
        name="gradient_blocks",
    )(cot, weight, slope, silu, proj, proj_x, block_d)


def score_kernel(scale, rows_ref, query_ref, out_ref):
    copies, sessions, width = out_ref.shape
    groups = query_ref.shape[0] // width
    grads = (rows_ref[:, 0] + rows_ref[:, 1]).reshape(sessions, -1)
    scores = lax.dot_general(
        grads,
        query_ref[...].astype(jnp.float32),
        (((1,), (1,)), ((), ())),
        precision=HIGHEST,
        preferred_element_type=jnp.float32,
    )
    scores = scores * scale
    for i in range(copies):
        first = i % groups * width
        out_ref[i] = scores[:, first : first + width]


def score_blocks(rows, query, copies, width, scale):
    return pl.pallas_call(
        functools.partial(score_kernel, scale),
        out_shape=jax.ShapeDtypeStruct((copies, rows.shape[0], width), jnp.float32),
        in_specs=[VMEM, VMEM],
        out_specs=VMEM,
        name="score_blocks",
    )(rows, query)


def give_all(block, axes):
    n = lax.axis_size(axes)
    return lax.all_to_all(jnp.broadcast_to(block[None], (n,) + block.shape), axes, 0, 0)


def on_device(
    inputs,
    cotangent,
    gate_pre,
    up_pre,
    down_weight,
    proj_in_x,
    proj_in_h,
    proj_out_ff,
    proj_out_d,
    queries,
    lengths,
):
    rows, width = cotangent.shape
    hid = gate_pre.shape[1]
    rank = proj_in_h.shape[1]
    own_yl = lax.axis_index("yl")
    tensor_size = lax.axis_size(TENSOR)

    weight = lax.all_gather(down_weight.T, ("zh", "zl", "c"), axis=0, tiled=True)

    halves = cotangent.reshape(rows, -1, 2, 2 * down_weight.shape[1])
    first, second = (halves[:, :, i].reshape(rows, width // 2) for i in (0, 1))
    mine = jnp.where(own_yl == 0, first, second)
    theirs = jnp.where(own_yl == 0, second, first)
    both_cot = jnp.concatenate([mine, lax.ppermute(theirs, "yl", SWAP)], axis=0)
    partner_pre = lax.ppermute(jnp.concatenate([gate_pre, up_pre], axis=0), "yl", SWAP)
    full_cot = give_all(both_cot, TENSOR)

    gate_float = jnp.concatenate([gate_pre, partner_pre[:rows]], axis=0).astype(jnp.float32)
    up_float = jnp.concatenate([up_pre, partner_pre[rows:]], axis=0).astype(jnp.float32)
    sig = jax.nn.sigmoid(gate_float)
    silu = gate_float * sig
    gate_slope = up_float * sig * (1.0 + gate_float * (1.0 - sig))
    own_gate = gate_pre.astype(jnp.float32)
    hidden = (own_gate * jax.nn.sigmoid(own_gate) * up_pre.astype(jnp.float32)).astype(jnp.bfloat16)

    groups = lax.axis_size(QUERY_GROUP)
    own_queries = queries.reshape(queries.shape[0], groups, -1).transpose(1, 0, 2)
    own_queries = lax.all_to_all(own_queries, QUERY_GROUP, 0, 0)
    own_queries = own_queries.reshape(groups * queries.shape[0], -1)

    parts = jnp.concatenate(
        [dot(inputs, proj_in_x), dot(hidden, proj_in_h), dot(cotangent, proj_out_d)], axis=1
    )
    some = rows // tensor_size
    sums = lax.all_to_all(parts.reshape(tensor_size, some, 4 * rank), TENSOR, 0, 0).sum(axis=0)
    first_event = lax.axis_index(DP) * rows + lax.axis_index(TENSOR) * some
    positions = first_event % LEN + jnp.arange(some, dtype=jnp.int32)
    live = (positions < lengths[first_event // LEN]).astype(jnp.float32)[:, None]
    sums_x, sums_h, sums_d = sums[:, : 2 * rank] * live, sums[:, 2 * rank : 3 * rank], sums[:, 3 * rank :]
    block_d = jnp.einsum("tr,ts->rs", sums_h, sums_d * live, precision=HIGHEST)
    proj_x = give_all(sums_x, ("yl",) + TENSOR).reshape(2, rows, 2 * rank)
    proj_x = jnp.where(own_yl == 0, proj_x, proj_x[::-1]).reshape(2 * rows, 2 * rank)

    members = tensor_size * groups
    blocks = gradient_blocks(full_cot, weight, gate_slope, silu, proj_out_ff, proj_x.T, block_d, members)

    entries = lax.all_to_all(blocks, SHARE, 0, 0).sum(axis=0)
    entries = give_all(entries, ("zh", "zl"))
    entries = entries.reshape(-1, lax.axis_size("zl"), *entries.shape[1:])
    partial_scores = score_blocks(entries, own_queries, members, queries.shape[0], 1.0 / math.sqrt(LEN))
    return lax.all_to_all(partial_scores, SHARE, 0, 0).sum(axis=0)


def solution(mesh):
    fine = Mesh(mesh.devices.reshape(8, 2, 2, 2, 4, 2), DP + TENSOR)
    return jax.shard_map(
        on_device,
        mesh=fine,
        in_specs=(
            P(DP, TENSOR),
            P(DP, TENSOR),
            P(DP, TENSOR),
            P(DP, TENSOR),
            P(TENSOR, DP),
            P(TENSOR, None),
            P(TENSOR, None),
            P(TENSOR, None),
            P(TENSOR, None),
            P(DP, TENSOR),
            P(),
        ),
        out_specs=P(None, DP),
        check_vma=False,
    )
```

```python
import functools
import math

import jax
import jax.numpy as jnp
from jax import lax
from jax.experimental import pallas as pl
from jax.experimental.pallas import tpu as pltpu
from jax.sharding import Mesh
from jax.sharding import PartitionSpec as P

LEN = 2048
TILE = 512
DP = ("zh", "zl", "yl", "c")
TENSOR = ("x", "yh")
QUERY_GROUP = ("yl", "c")
SHARE = TENSOR + QUERY_GROUP
SWAP = [(0, 1), (1, 0)]
HIGHEST = lax.Precision.HIGHEST
VMEM = pl.BlockSpec(memory_space=pltpu.VMEM)


def dot(a, b):
    return jnp.dot(a, b, preferred_element_type=jnp.float32)


def gradient_kernel(
    cot_ref, weight_ref, slope_ref, silu_ref, proj_ref, x_ref, down_ref, _, out_ref, held, part, rows_ref, sems
):
    hid = slope_ref.shape[1]
    rank = down_ref.shape[0]
    chunks = sems.shape[0]
    depth = weight_ref.shape[0]
    span = depth // chunks
    copies = [
        pltpu.make_async_copy(weight_ref.at[pl.ds(i * span, span)], held.at[pl.ds(i * span, span)], sems.at[i])
        for i in range(chunks)
    ]
    for copy in copies:
        copy.start()
    tiles = [slice(start, min(start + TILE, hid)) for start in range(0, hid, TILE)]
    half = depth // 2
    for copy in copies[: chunks // 2]:
        copy.wait()
    for tile in tiles:
        part[:, tile] = dot(cot_ref[:, :half], held[:half, tile])
    for copy in copies[chunks // 2 :]:
        copy.wait()
    gate_sum = up_sum = None
    for tile in tiles:
        grad = part[:, tile] + dot(cot_ref[:, half:], held[half:, tile])
        proj = proj_ref[tile, :]
        gate_term = dot((grad * slope_ref[:, tile].astype(jnp.float32)).astype(jnp.bfloat16), proj)
        up_term = dot((grad * silu_ref[:, tile].astype(jnp.float32)).astype(jnp.bfloat16), proj)
        gate_sum = gate_term if gate_sum is None else gate_sum + gate_term
        up_sum = up_term if up_sum is None else up_sum + up_term
    lane = lax.broadcasted_iota(jnp.int32, gate_sum.shape, 1)
    both = jnp.where(lane < rank, gate_sum, up_sum)
    square = jnp.dot(x_ref[...], both, precision=HIGHEST, preferred_element_type=jnp.float32)
    rows_ref[:rank, :rank] = square[:rank, :rank]
    rows_ref[rank : 2 * rank, :rank] = square[rank:, rank:]
    rows_ref[2 * rank :, :rank] = down_ref[...]
    rows_ref[:, rank:] = jnp.zeros_like(rows_ref[:, rank:])
    members = out_ref.shape[0]
    each = rows_ref.shape[0] // members
    for i in range(each):
        row = rows_ref[pl.ds(i, members, stride=each), :]
        out_ref[:, :, i * rank : (i + 1) * rank] = row[:, None, :rank]


def gradient_blocks(cot, weight, slope, silu, proj, proj_x, block_d, queries, members):
    rank = block_d.shape[0]
    anywhere = pl.BlockSpec(memory_space=pl.ANY)
    return pl.pallas_call(
        gradient_kernel,
        out_shape=jax.ShapeDtypeStruct((members, 1, 3 * rank * rank // members), jnp.float32),
        in_specs=[VMEM, anywhere] + [VMEM] * 5 + [anywhere],
        out_specs=VMEM,
        scratch_shapes=[
            pltpu.VMEM(weight.shape, jnp.bfloat16),
            pltpu.VMEM(slope.shape, jnp.float32),
            pltpu.VMEM((3 * rank, 2 * rank), jnp.float32),
            pltpu.SemaphoreType.DMA((4,)),
        ],
        compiler_params=pltpu.CompilerParams(vmem_limit_bytes=54 * 2**20),
        cost_estimate=pl.CostEstimate(
            flops=2 * slope.shape[0] * weight.shape[0] * weight.shape[1],
            bytes_accessed=weight.size * 2,
            transcendentals=0,
        ),
        name="gradient_blocks",
    )(cot, weight, slope, silu, proj, proj_x, block_d, queries)


def score_kernel(scale, rows_ref, query_ref, out_ref):
    copies, sessions, width = out_ref.shape
    groups = query_ref.shape[1] // width
    left = (rows_ref[:, 0] + rows_ref[:, 1]).reshape(sessions, -1)
    terms = []
    for _ in range(3):
        terms.append(left.astype(jnp.bfloat16).astype(jnp.float32))
        left = left - terms[-1]
    products = dot(jnp.concatenate(terms, axis=0).astype(jnp.bfloat16), query_ref[...])
    scores = products[:sessions] + (products[sessions : 2 * sessions] + products[2 * sessions :])
    scores = scores * scale
    for i in range(copies):
        first = i % groups * width
        out_ref[i] = scores[:, first : first + width]


def score_blocks(rows, query, copies, width, scale):
    return pl.pallas_call(
        functools.partial(score_kernel, scale),
        out_shape=jax.ShapeDtypeStruct((copies, rows.shape[0], width), jnp.float32),
        in_specs=[VMEM, VMEM],
        out_specs=VMEM,
        name="score_blocks",
    )(rows, query)


def give_all(block, axes):
    n = lax.axis_size(axes)
    return lax.all_to_all(jnp.broadcast_to(block[None], (n,) + block.shape), axes, 0, 0)


def on_device(
    inputs,
    cotangent,
    gate_pre,
    up_pre,
    down_weight,
    proj_in_x,
    proj_in_h,
    proj_out_ff,
    proj_out_d,
    queries,
    lengths,
):
    rows, width = cotangent.shape
    hid = gate_pre.shape[1]
    rank = proj_in_h.shape[1]
    own_yl = lax.axis_index("yl")
    tensor_size = lax.axis_size(TENSOR)

    weight = lax.all_gather(down_weight.T, ("zh", "zl", "c"), axis=0, tiled=True)

    per_half = cotangent.reshape(rows, -1, 2, 2 * down_weight.shape[1]).transpose(2, 0, 1, 3)
    per_half = per_half.reshape(2, 1, rows, width // 2)
    pieces = jnp.broadcast_to(per_half, (2, tensor_size, rows, width // 2))
    full_cot = lax.all_to_all(pieces.reshape(-1, rows, width // 2), ("yl",) + TENSOR, 0, 0)
    full_cot = full_cot.reshape(2, tensor_size, rows, width // 2).transpose(0, 2, 1, 3)
    full_cot = full_cot.reshape(2 * rows, -1)

    partner_pre = lax.ppermute(jnp.concatenate([gate_pre, up_pre], axis=0), "yl", SWAP)

    def in_order(own, partner):
        swapped = own_yl == 1
        return jnp.concatenate([jnp.where(swapped, partner, own), jnp.where(swapped, own, partner)], axis=0)

    gate_float = in_order(gate_pre, partner_pre[:rows]).astype(jnp.float32)
    up_float = in_order(up_pre, partner_pre[rows:]).astype(jnp.float32)
    sig = jax.nn.sigmoid(gate_float)
    silu = (gate_float * sig).astype(jnp.bfloat16)
    gate_slope = (up_float * sig * (1.0 + gate_float * (1.0 - sig))).astype(jnp.bfloat16)
    own_gate = gate_pre.astype(jnp.float32)
    hidden = (own_gate * jax.nn.sigmoid(own_gate) * up_pre.astype(jnp.float32)).astype(jnp.bfloat16)

    groups = lax.axis_size(QUERY_GROUP)
    member = lax.axis_index(QUERY_GROUP)
    quarters = queries.reshape(queries.shape[0], groups, -1).transpose(1, 0, 2)
    arrivals = []
    for flip in range(groups):
        piece = lax.dynamic_index_in_dim(quarters, member ^ flip, 0, keepdims=False)
        pairs = [(i, i ^ flip) for i in range(groups)]
        arrivals.append(lax.ppermute(piece, QUERY_GROUP, pairs) if flip else piece)
    for bit in (1, 2):
        arrivals = [jnp.where(member & bit, arrivals[i ^ bit], arrivals[i]) for i in range(groups)]
    own_queries = jnp.concatenate(arrivals, axis=0).T

    parts = jnp.concatenate(
        [dot(inputs, proj_in_x), dot(hidden, proj_in_h), dot(cotangent, proj_out_d)], axis=1
    )
    parts, full_cot = lax.optimization_barrier((parts, full_cot))
    some = rows // tensor_size
    sums = lax.all_to_all(parts.reshape(tensor_size, some, 4 * rank), TENSOR, 0, 0).sum(axis=0)
    first_event = lax.axis_index(DP) * rows + lax.axis_index(TENSOR) * some
    positions = first_event % LEN + jnp.arange(some, dtype=jnp.int32)
    live = (positions < lengths[first_event // LEN]).astype(jnp.float32)[:, None]
    sums_x, sums_h, sums_d = sums[:, : 2 * rank] * live, sums[:, 2 * rank : 3 * rank], sums[:, 3 * rank :]
    block_d = jnp.einsum("tr,ts->rs", sums_h, sums_d * live, precision=HIGHEST)
    proj_x = give_all(sums_x, ("yl",) + TENSOR).reshape(2 * rows, 2 * rank)

    members = tensor_size * groups
    blocks = gradient_blocks(
        full_cot, weight, gate_slope, silu, proj_out_ff, proj_x.T, block_d, own_queries, members
    )

    entries = lax.all_to_all(blocks, SHARE, 0, 0).sum(axis=0)
    entries = give_all(entries, ("zh", "zl"))
    entries = entries.reshape(-1, lax.axis_size("zl"), *entries.shape[1:])
    partial_scores = score_blocks(entries, own_queries, members, queries.shape[0], 1.0 / math.sqrt(LEN))
    return lax.all_to_all(partial_scores, SHARE, 0, 0).sum(axis=0)


def solution(mesh):
    fine = Mesh(mesh.devices.reshape(8, 2, 2, 2, 4, 2), DP + TENSOR)
    return jax.shard_map(
        on_device,
        mesh=fine,
        in_specs=(
            P(DP, TENSOR),
            P(DP, TENSOR),
            P(DP, TENSOR),
            P(DP, TENSOR),
            P(TENSOR, DP),
            P(TENSOR, None),
            P(TENSOR, None),
            P(TENSOR, None),
            P(TENSOR, None),
            P(DP, TENSOR),
            P(),
        ),
        out_specs=P(None, DP),
        check_vma=False,
    )
```

```python
import functools
import math

import jax
import jax.numpy as jnp
from jax import lax
from jax.experimental import pallas as pl
from jax.experimental.pallas import tpu as pltpu
from jax.sharding import Mesh
from jax.sharding import PartitionSpec as P

LEN = 2048
STEP = 32
CHUNKS = 4
DP = ("zh", "zl", "yl", "c")
TENSOR = ("x", "yh")
QUERY_GROUP = ("yl", "c")
SHARE = TENSOR + QUERY_GROUP
SWAP = [(0, 1), (1, 0)]
HIGHEST = lax.Precision.HIGHEST
VMEM = pl.BlockSpec(memory_space=pltpu.VMEM)


def dot(a, b):
    return jnp.dot(a, b, preferred_element_type=jnp.float32)


def prepare_kernel(yl_ref, blocks_ref, own_ref, partner_ref, cot_ref, slope_ref, silu_ref):
    across, _, along, rows, depth = blocks_ref.shape
    yl = yl_ref[0]
    for i, source in enumerate((yl, 1 - yl)):
        for x in range(across):
            for y in range(along):
                start = (x * along + y) * depth
                cot_ref[i * rows : (i + 1) * rows, start : start + depth] = blocks_ref[x, source, y]
    for i, pre_ref in enumerate((own_ref, partner_ref)):

        def some_rows(step, _, i=i, pre_ref=pre_ref):
            first = pl.multiple_of(step * STEP, STEP)
            gate = pre_ref[pl.ds(first, STEP), :].astype(jnp.float32)
            up = pre_ref[pl.ds(rows + first, STEP), :].astype(jnp.float32)
            sig = 1.0 / (1.0 + jnp.exp(-gate))
            here = pl.ds(i * rows + first, STEP)
            silu_ref[here, :] = (gate * sig).astype(jnp.bfloat16)
            slope_ref[here, :] = (up * sig * (1.0 + gate * (1.0 - sig))).astype(jnp.bfloat16)
            return 0

        lax.fori_loop(0, rows // STEP, some_rows, 0)


def prepare(yl, blocks, own, partner):
    rows, depth = blocks.shape[3:]
    hid = own.shape[1]
    return pl.pallas_call(
        prepare_kernel,
        out_shape=(
            jax.ShapeDtypeStruct((2 * rows, blocks.shape[0] * blocks.shape[2] * depth), jnp.bfloat16),
            jax.ShapeDtypeStruct((2 * rows, hid), jnp.bfloat16),
            jax.ShapeDtypeStruct((2 * rows, hid), jnp.bfloat16),
        ),
        in_specs=[pl.BlockSpec(memory_space=pltpu.SMEM)] + [VMEM] * 3,
        out_specs=(VMEM,) * 3,
        compiler_params=pltpu.CompilerParams(vmem_limit_bytes=56 * 2**20),
        cost_estimate=pl.CostEstimate(flops=20 * rows * hid, bytes_accessed=8 * rows * hid, transcendentals=4 * rows * hid),
        name="prepare",
    )(yl, blocks, own, partner)


def gradient_kernel(
    yl_ref, cot_hbm, weight_hbm, slope_hbm, silu_hbm, proj_ref, x_ref, down_ref, _,
    out_ref, cot, weight, slope, silu, total, rows_ref, sems,
):
    rank = down_ref.shape[0]
    span = weight.shape[0] // CHUNKS
    chunks = [pl.ds(i * span, span) for i in range(CHUNKS)]
    moves = [(cot_hbm, cot)] + [(weight_hbm.at[chunk], weight.at[chunk]) for chunk in chunks]
    moves += [(slope_hbm, slope), (silu_hbm, silu)]
    copies = [pltpu.make_async_copy(source, target, sems.at[i]) for i, (source, target) in enumerate(moves)]
    for copy in copies:
        copy.start()
    copies[0].wait()
    for i, chunk in enumerate(chunks):
        copies[1 + i].wait()
        term = dot(cot[:, chunk], weight[chunk, :])
        if i == 0:
            total[...] = term
        elif i < CHUNKS - 1:
            total[...] += term
    grad = total[...] + term
    copies[-2].wait()
    copies[-1].wait()
    gate_sum = dot((grad * slope[...].astype(jnp.float32)).astype(jnp.bfloat16), proj_ref[...])
    up_sum = dot((grad * silu[...].astype(jnp.float32)).astype(jnp.bfloat16), proj_ref[...])
    lane = lax.broadcasted_iota(jnp.int32, gate_sum.shape, 1)
    both = jnp.where(lane < rank, gate_sum, up_sum)
    events = x_ref.shape[2]
    yl = yl_ref[0]
    square = jnp.dot(x_ref[yl], both[:events], precision=HIGHEST, preferred_element_type=jnp.float32)
    square += jnp.dot(x_ref[1 - yl], both[events:], precision=HIGHEST, preferred_element_type=jnp.float32)
    rows_ref[:rank, :rank] = square[:rank, :rank]
    rows_ref[rank : 2 * rank, :rank] = square[rank:, rank:]
    rows_ref[2 * rank :, :rank] = down_ref[...]
    rows_ref[:, rank:] = jnp.zeros_like(rows_ref[:, rank:])
    members = out_ref.shape[0]
    each = rows_ref.shape[0] // members
    for i in range(each):
        row = rows_ref[pl.ds(i, members, stride=each), :]
        out_ref[:, :, i * rank : (i + 1) * rank] = row[:, None, :rank]


def gradient_blocks(yl, cot, weight, slope, silu, proj, proj_x, block_d, queries, members):
    rank = block_d.shape[0]
    anywhere = pl.BlockSpec(memory_space=pl.ANY)
    return pl.pallas_call(
        gradient_kernel,
        out_shape=jax.ShapeDtypeStruct((members, 1, 3 * rank * rank // members), jnp.float32),
        in_specs=[pl.BlockSpec(memory_space=pltpu.SMEM)] + [anywhere] * 4 + [VMEM] * 3 + [anywhere],
        out_specs=VMEM,
        scratch_shapes=[
            pltpu.VMEM(cot.shape, jnp.bfloat16),
            pltpu.VMEM(weight.shape, jnp.bfloat16),
            pltpu.VMEM(slope.shape, jnp.bfloat16),
            pltpu.VMEM(silu.shape, jnp.bfloat16),
            pltpu.VMEM(slope.shape, jnp.float32),
            pltpu.VMEM((3 * rank, 2 * rank), jnp.float32),
            pltpu.SemaphoreType.DMA((CHUNKS + 3,)),
        ],
        compiler_params=pltpu.CompilerParams(vmem_limit_bytes=56 * 2**20),
        cost_estimate=pl.CostEstimate(
            flops=2 * slope.shape[0] * weight.shape[0] * weight.shape[1],
            bytes_accessed=weight.size * 2,
            transcendentals=0,
        ),
        name="gradient_blocks",
    )(yl, cot, weight, slope, silu, proj, proj_x, block_d, queries)


def score_kernel(scale, rows_ref, query_ref, out_ref):
    copies, sessions, width = out_ref.shape
    groups = query_ref.shape[1] // width
    left = (rows_ref[:, 0] + rows_ref[:, 1]).reshape(sessions, -1)
    terms = []
    for _ in range(3):
        terms.append(left.astype(jnp.bfloat16).astype(jnp.float32))
        left = left - terms[-1]
    products = dot(jnp.concatenate(terms, axis=0).astype(jnp.bfloat16), query_ref[...])
    scores = products[:sessions] + (products[sessions : 2 * sessions] + products[2 * sessions :])
    scores = scores * scale
    for i in range(copies):
        first = i % groups * width
        out_ref[i] = scores[:, first : first + width]


def score_blocks(rows, query, copies, width, scale):
    return pl.pallas_call(
        functools.partial(score_kernel, scale),
        out_shape=jax.ShapeDtypeStruct((copies, rows.shape[0], width), jnp.float32),
        in_specs=[VMEM, VMEM],
        out_specs=VMEM,
        name="score_blocks",
    )(rows, query)


def give_all(block, axes):
    n = lax.axis_size(axes)
    return lax.all_to_all(jnp.broadcast_to(block[None], (n,) + block.shape), axes, 0, 0)


def on_device(
    inputs,
    cotangent,
    gate_pre,
    up_pre,
    down_weight,
    proj_in_x,
    proj_in_h,
    proj_out_ff,
    proj_out_d,
    queries,
    lengths,
):
    rows, width = cotangent.shape
    hid = gate_pre.shape[1]
    rank = proj_in_h.shape[1]
    own_yl = lax.axis_index("yl")
    tensor_size = lax.axis_size(TENSOR)

    weight = lax.all_gather(down_weight.T, ("zh", "zl", "c"), axis=0, tiled=True)

    per_half = cotangent.reshape(rows, -1, 2, 2 * down_weight.shape[1]).transpose(2, 0, 1, 3)
    per_half = per_half.reshape(2, 1, rows, width // 2)
    per_half = jnp.broadcast_to(per_half, (2, lax.axis_size("yh"), rows, width // 2))
    along_y = lax.all_to_all(per_half.reshape(-1, rows, width // 2), ("yl", "yh"), 0, 0)

    own_gate = gate_pre.astype(jnp.float32)
    hidden = (own_gate * jax.nn.sigmoid(own_gate) * up_pre.astype(jnp.float32)).astype(jnp.bfloat16)
    parts = jnp.concatenate(
        [dot(inputs, proj_in_x), dot(hidden, proj_in_h), dot(cotangent, proj_out_d)], axis=1
    )

    both_pre = jnp.concatenate([gate_pre, up_pre], axis=0)
    along_y = jnp.broadcast_to(along_y[None], (lax.axis_size("x"),) + along_y.shape)
    along_y, both_pre, queries = lax.optimization_barrier((along_y, both_pre, queries))
    along_x = lax.all_to_all(along_y, "x", 0, 0).reshape(-1, 2, lax.axis_size("yh"), rows, width // 2)

    groups = lax.axis_size(QUERY_GROUP)
    member = lax.axis_index(QUERY_GROUP)
    quarters = queries.reshape(queries.shape[0], groups, -1).transpose(1, 0, 2)
    arrivals = []
    for flip in range(groups):
        piece = lax.dynamic_index_in_dim(quarters, member ^ flip, 0, keepdims=False)
        pairs = [(i, i ^ flip) for i in range(groups)]
        arrivals.append(lax.ppermute(piece, QUERY_GROUP, pairs) if flip else piece)

    partner_pre = lax.ppermute(both_pre, "yl", SWAP)
    yl = own_yl.reshape(1)
    full_cot, gate_slope, silu = prepare(yl, along_x, both_pre, partner_pre)

    some = rows // tensor_size
    parts, along_x = lax.optimization_barrier((parts, along_x))
    sums = lax.all_to_all(parts.reshape(tensor_size, some, 4 * rank), TENSOR, 0, 0).sum(axis=0)

    first_event = lax.axis_index(DP) * rows + lax.axis_index(TENSOR) * some
    positions = first_event % LEN + jnp.arange(some, dtype=jnp.int32)
    live = (positions < lengths[first_event // LEN]).astype(jnp.float32)[:, None]
    sums_x, sums_h, sums_d = sums[:, : 2 * rank] * live, sums[:, 2 * rank : 3 * rank], sums[:, 3 * rank :]
    block_d = jnp.einsum("tr,ts->rs", sums_h, sums_d * live, precision=HIGHEST)
    proj_x = give_all(sums_x, ("yl",) + TENSOR).reshape(2, rows, 2 * rank).transpose(0, 2, 1)

    proj_x, arrivals = lax.optimization_barrier((proj_x, arrivals))
    for bit in (1, 2):
        arrivals = [jnp.where(member & bit, arrivals[i ^ bit], arrivals[i]) for i in range(groups)]
    own_queries = jnp.concatenate(arrivals, axis=0).T

    members = tensor_size * groups
    blocks = gradient_blocks(
        yl, full_cot, weight, gate_slope, silu, proj_out_ff, proj_x, block_d, own_queries, members
    )

    entries = lax.all_to_all(blocks, SHARE, 0, 0).sum(axis=0)
    entries = give_all(entries, ("zh", "zl"))
    entries = entries.reshape(-1, lax.axis_size("zl"), *entries.shape[1:])
    partial_scores = score_blocks(entries, own_queries, members, queries.shape[0], 1.0 / math.sqrt(LEN))
    return lax.all_to_all(partial_scores, SHARE, 0, 0).sum(axis=0)


def solution(mesh):
    fine = Mesh(mesh.devices.reshape(8, 2, 2, 2, 4, 2), DP + TENSOR)
    return jax.shard_map(
        on_device,
        mesh=fine,
        in_specs=(
            P(DP, TENSOR),
            P(DP, TENSOR),
            P(DP, TENSOR),
            P(DP, TENSOR),
            P(TENSOR, DP),
            P(TENSOR, None),
            P(TENSOR, None),
            P(TENSOR, None),
            P(TENSOR, None),
            P(DP, TENSOR),
            P(),
        ),
        out_specs=P(None, DP),
        check_vma=False,
    )
```

```python
import functools
import math

import jax
import jax.numpy as jnp
from jax import lax
from jax.experimental import pallas as pl
from jax.experimental.pallas import tpu as pltpu
from jax.sharding import Mesh
from jax.sharding import PartitionSpec as P

LEN = 2048
STEP = 32
CHUNKS = 4
DP = ("zh", "zl", "yl", "c")
TENSOR = ("x", "yh")
QUERY_GROUP = ("yl", "c")
SHARE = TENSOR + QUERY_GROUP
SWAP = [(0, 1), (1, 0)]
HIGHEST = lax.Precision.HIGHEST
VMEM = pl.BlockSpec(memory_space=pltpu.VMEM)


def dot(a, b):
    return jnp.dot(a, b, preferred_element_type=jnp.float32)


def local_kernel(pre_ref, in_ref, in_proj_ref, hid_proj_ref, cot_ref, out_proj_ref, slopes_ref, parts_ref, hidden_ref):
    rows = hidden_ref.shape[0]
    rank = out_proj_ref.shape[1]

    def some_rows(step, _):
        first = pl.multiple_of(step * STEP, STEP)
        above, below = pl.ds(first, STEP), pl.ds(rows + first, STEP)
        gate = pre_ref[above, :].astype(jnp.float32)
        up = pre_ref[below, :].astype(jnp.float32)
        sig = 1.0 / (1.0 + jnp.exp(-gate))
        silu = gate * sig
        slopes_ref[above, :] = (up * sig * (1.0 + gate * (1.0 - sig))).astype(jnp.bfloat16)
        slopes_ref[below, :] = silu.astype(jnp.bfloat16)
        hidden_ref[above, :] = (silu * up).astype(jnp.bfloat16)
        return 0

    lax.fori_loop(0, rows // STEP, some_rows, 0)
    parts_ref[:, : 2 * rank] = dot(in_ref[...], in_proj_ref[...])
    parts_ref[:, 2 * rank : 3 * rank] = dot(hidden_ref[...], hid_proj_ref[...])
    parts_ref[:, 3 * rank :] = dot(cot_ref[...], out_proj_ref[...])


def local_terms(pre, inputs, proj_in_x, proj_in_h, cotangent, proj_out_d):
    rows, hid = pre.shape[0] // 2, pre.shape[1]
    return pl.pallas_call(
        local_kernel,
        out_shape=(
            jax.ShapeDtypeStruct((2 * rows, hid), jnp.bfloat16),
            jax.ShapeDtypeStruct((rows, 4 * proj_out_d.shape[1]), jnp.float32),
        ),
        in_specs=[VMEM] * 6,
        out_specs=(VMEM, VMEM),
        scratch_shapes=[pltpu.VMEM((rows, hid), jnp.bfloat16)],
        compiler_params=pltpu.CompilerParams(vmem_limit_bytes=56 * 2**20),
        cost_estimate=pl.CostEstimate(flops=800 * rows * hid, bytes_accessed=8 * rows * hid, transcendentals=2 * rows * hid),
        name="local_terms",
    )(pre, inputs, proj_in_x, proj_in_h, cotangent, proj_out_d)


def gradient_kernel(
    yl_ref, blocks_hbm, weight_hbm, own_slopes, partner_slopes, proj_ref, x_ref, down_ref, _,
    out_ref, cot, weight, slope, silu, total, rows_ref, sems,
):
    rank = down_ref.shape[0]
    across, _, along, events, depth = blocks_hbm.shape
    span = weight.shape[0] // CHUNKS
    chunks = [pl.ds(i * span, span) for i in range(CHUNKS)]
    yl = yl_ref[0]
    own, partner = pl.ds(0, events), pl.ds(events, events)
    cot_moves = [
        (blocks_hbm.at[x, source, y], cot.at[rows, pl.ds((x * along + y) * depth, depth)])
        for x in range(across)
        for y in range(along)
        for source, rows in ((yl, own), (1 - yl, partner))
    ]
    weight_moves = [(weight_hbm.at[chunk], weight.at[chunk]) for chunk in chunks]
    above, below = own, partner
    slope_moves = [(own_slopes.at[above], slope.at[own]), (partner_slopes.at[above], slope.at[partner])]
    slope_moves += [(own_slopes.at[below], silu.at[own]), (partner_slopes.at[below], silu.at[partner])]
    per_chunk = len(cot_moves) // CHUNKS
    copies = []
    for source, target in cot_moves + weight_moves + slope_moves:
        copies.append(pltpu.make_async_copy(source, target, sems.at[len(copies)]))
    of_cot, of_weight = copies[: len(cot_moves)], copies[len(cot_moves) :][:CHUNKS]
    of_slopes = copies[len(cot_moves) + CHUNKS :]
    for i in range(CHUNKS):
        for copy in of_cot[i * per_chunk :][:per_chunk]:
            copy.start()
        of_weight[i].start()
    for copy in of_slopes:
        copy.start()
    for i, chunk in enumerate(chunks):
        for copy in of_cot[i * per_chunk :][:per_chunk]:
            copy.wait()
        of_weight[i].wait()
        term = dot(cot[:, chunk], weight[chunk, :])
        if i == 0:
            total[...] = term
        elif i < CHUNKS - 1:
            total[...] += term
    grad = total[...] + term
    for copy in of_slopes:
        copy.wait()
    gate_sum = dot((grad * slope[...].astype(jnp.float32)).astype(jnp.bfloat16), proj_ref[...])
    up_sum = dot((grad * silu[...].astype(jnp.float32)).astype(jnp.bfloat16), proj_ref[...])
    lane = lax.broadcasted_iota(jnp.int32, gate_sum.shape, 1)
    both = jnp.where(lane < rank, gate_sum, up_sum)
    square = outer(x_ref[yl], both[:events]) + outer(x_ref[1 - yl], both[events:])
    rows_ref[:rank, :rank] = square[:rank, :rank]
    rows_ref[rank : 2 * rank, :rank] = square[rank:, rank:]
    rows_ref[2 * rank :, :rank] = down_ref[...]
    rows_ref[:, rank:] = jnp.zeros_like(rows_ref[:, rank:])
    members = out_ref.shape[0]
    each = rows_ref.shape[0] // members
    for i in range(each):
        row = rows_ref[pl.ds(i, members, stride=each), :]
        out_ref[:, :, i * rank : (i + 1) * rank] = row[:, None, :rank]


def gradient_blocks(yl, blocks, weight, own_slopes, partner_slopes, proj, proj_x, block_d, arrival, members):
    rank = block_d.shape[0]
    rows, hid = 2 * blocks.shape[3], weight.shape[1]
    depth = weight.shape[0]
    anywhere = pl.BlockSpec(memory_space=pl.ANY)
    return pl.pallas_call(
        gradient_kernel,
        out_shape=jax.ShapeDtypeStruct((members, 1, 3 * rank * rank // members), jnp.float32),
        in_specs=[pl.BlockSpec(memory_space=pltpu.SMEM)] + [anywhere] * 4 + [VMEM] * 3 + [anywhere],
        out_specs=VMEM,
        scratch_shapes=[
            pltpu.VMEM((rows, depth), jnp.bfloat16),
            pltpu.VMEM((depth, hid), jnp.bfloat16),
            pltpu.VMEM((rows, hid), jnp.bfloat16),
            pltpu.VMEM((rows, hid), jnp.bfloat16),
            pltpu.VMEM((rows, hid), jnp.float32),
            pltpu.VMEM((3 * rank, 2 * rank), jnp.float32),
            pltpu.SemaphoreType.DMA((blocks.shape[0] * 2 * blocks.shape[2] + CHUNKS + 4,)),
        ],
        compiler_params=pltpu.CompilerParams(vmem_limit_bytes=56 * 2**20),
        cost_estimate=pl.CostEstimate(
            flops=2 * rows * depth * hid,
            bytes_accessed=weight.size * 2,
            transcendentals=0,
        ),
        name="gradient_blocks",
    )(yl, blocks, weight, own_slopes, partner_slopes, proj, proj_x, block_d, arrival)


def score_kernel(scale, member_ref, rows_ref, query_ref, out_ref):
    copies, sessions, _ = out_ref.shape
    groups = query_ref.shape[0]
    left = (rows_ref[:, 0] + rows_ref[:, 1]).reshape(sessions, -1)
    terms = []
    for _ in range(3):
        terms.append(left.astype(jnp.bfloat16).astype(jnp.float32))
        left = left - terms[-1]
    terms = jnp.concatenate(terms, axis=0).astype(jnp.bfloat16)
    for group in range(groups):
        products = dot(terms, query_ref[member_ref[0] ^ group])
        scores = products[:sessions] + (products[sessions : 2 * sessions] + products[2 * sessions :])
        for i in range(group, copies, groups):
            out_ref[i] = scores * scale


def score_blocks(member, rows, query, copies, scale):
    return pl.pallas_call(
        functools.partial(score_kernel, scale),
        out_shape=jax.ShapeDtypeStruct((copies, rows.shape[0], query.shape[2]), jnp.float32),
        in_specs=[pl.BlockSpec(memory_space=pltpu.SMEM), VMEM, VMEM],
        out_specs=VMEM,
        name="score_blocks",
    )(member, rows, query)


def outer(a, b):
    return lax.dot_general(
        a, b, (((0,), (0,)), ((), ())), precision=HIGHEST, preferred_element_type=jnp.float32
    )


def give_all(block, axes):
    n = lax.axis_size(axes)
    return lax.all_to_all(jnp.broadcast_to(block[None], (n,) + block.shape), axes, 0, 0)


def on_device(
    inputs,
    cotangent,
    gate_pre,
    up_pre,
    down_weight,
    proj_in_x,
    proj_in_h,
    proj_out_ff,
    proj_out_d,
    queries,
    lengths,
):
    rows, width = cotangent.shape
    hid = gate_pre.shape[1]
    rank = proj_in_h.shape[1]
    own_yl = lax.axis_index("yl")
    tensor_size = lax.axis_size(TENSOR)

    weight = lax.all_gather(down_weight.T, ("zh", "zl", "c"), axis=0, tiled=True)

    per_half = cotangent.reshape(rows, -1, 2, 2 * down_weight.shape[1]).transpose(2, 0, 1, 3)
    per_half = per_half.reshape(2, 1, rows, width // 2)
    per_half = jnp.broadcast_to(per_half, (2, lax.axis_size("yh"), rows, width // 2))
    along_y = lax.all_to_all(per_half.reshape(-1, rows, width // 2), ("yl", "yh"), 0, 0)

    both_pre = jnp.concatenate([gate_pre, up_pre], axis=0)
    own_slopes, parts = local_terms(both_pre, inputs, proj_in_x, proj_in_h, cotangent, proj_out_d)

    along_y = jnp.broadcast_to(along_y[None], (lax.axis_size("x"),) + along_y.shape)
    along_y, own_slopes = lax.optimization_barrier((along_y, own_slopes))
    along_x = lax.all_to_all(along_y, "x", 0, 0).reshape(-1, 2, lax.axis_size("yh"), rows, width // 2)

    partner_slopes = lax.ppermute(own_slopes, "yl", SWAP)

    groups = lax.axis_size(QUERY_GROUP)
    member = lax.axis_index(QUERY_GROUP)
    quarters = queries.T.reshape(groups, -1, queries.shape[0])
    arrivals = []
    for flip in range(groups):
        piece = lax.dynamic_index_in_dim(quarters, member ^ flip, 0, keepdims=False)
        pairs = [(i, i ^ flip) for i in range(groups)]
        arrivals.append(lax.ppermute(piece, QUERY_GROUP, pairs) if flip else piece)

    yl = own_yl.reshape(1)

    some = rows // tensor_size
    parts, along_x = lax.optimization_barrier((parts, along_x))
    sums = lax.all_to_all(parts.reshape(tensor_size, some, 4 * rank), TENSOR, 0, 0).sum(axis=0)

    sums, arrivals[1], arrivals[2] = lax.optimization_barrier((sums, arrivals[1], arrivals[2]))
    first_event = lax.axis_index(DP) * rows + lax.axis_index(TENSOR) * some
    positions = first_event % LEN + jnp.arange(some, dtype=jnp.int32)
    live = (positions < lengths[first_event // LEN]).astype(jnp.float32)[:, None]
    sums_x, sums_h, sums_d = sums[:, : 2 * rank] * live, sums[:, 2 * rank : 3 * rank], sums[:, 3 * rank :]
    block_d = jnp.einsum("tr,ts->rs", sums_h, sums_d * live, precision=HIGHEST)
    proj_x = give_all(sums_x, ("yl",) + TENSOR).reshape(2, rows, 2 * rank)

    proj_x, arrivals[3] = lax.optimization_barrier((proj_x, arrivals[3]))

    members = tensor_size * groups
    blocks = gradient_blocks(
        yl, along_x, weight, own_slopes, partner_slopes, proj_out_ff, proj_x, block_d, arrivals[3], members
    )

    entries = lax.all_to_all(blocks, SHARE, 0, 0).sum(axis=0)
    entries = give_all(entries, ("zh", "zl"))
    entries = entries.reshape(-1, lax.axis_size("zl"), *entries.shape[1:])
    partial_scores = score_blocks(member.reshape(1), entries, jnp.stack(arrivals), members, 1.0 / math.sqrt(LEN))
    return lax.all_to_all(partial_scores, SHARE, 0, 0).sum(axis=0)


def solution(mesh):
    fine = Mesh(mesh.devices.reshape(8, 2, 2, 2, 4, 2), DP + TENSOR)
    return jax.shard_map(
        on_device,
        mesh=fine,
        in_specs=(
            P(DP, TENSOR),
            P(DP, TENSOR),
            P(DP, TENSOR),
            P(DP, TENSOR),
            P(TENSOR, DP),
            P(TENSOR, None),
            P(TENSOR, None),
            P(TENSOR, None),
            P(TENSOR, None),
            P(DP, TENSOR),
            P(),
        ),
        out_specs=P(None, DP),
        check_vma=False,
    )
```

```python
import functools
import math

import jax
import jax.numpy as jnp
from jax import lax
from jax.experimental import pallas as pl
from jax.experimental.pallas import tpu as pltpu
from jax.sharding import Mesh
from jax.sharding import PartitionSpec as P

LEN = 2048
STEP = 32
CHUNKS = 4
DP = ("zh", "zl", "yl", "c")
TENSOR = ("x", "yh")
QUERY_GROUP = ("yl", "c")
SHARE = TENSOR + QUERY_GROUP
SWAP = [(0, 1), (1, 0)]
HIGHEST = lax.Precision.HIGHEST
VMEM = pl.BlockSpec(memory_space=pltpu.VMEM)


def dot(a, b):
    return jnp.dot(a, b, preferred_element_type=jnp.float32)


def local_kernel(pre_ref, in_ref, in_proj_ref, hid_proj_ref, cot_ref, out_proj_ref, slopes_ref, parts_ref, hidden_ref):
    rows = hidden_ref.shape[0]
    rank = out_proj_ref.shape[1]

    def some_rows(step, _):
        first = pl.multiple_of(step * STEP, STEP)
        above, below = pl.ds(first, STEP), pl.ds(rows + first, STEP)
        gate = pre_ref[above, :].astype(jnp.float32)
        up = pre_ref[below, :].astype(jnp.float32)
        sig = 1.0 / (1.0 + jnp.exp(-gate))
        silu = gate * sig
        slopes_ref[above, :] = (up * sig * (1.0 + gate * (1.0 - sig))).astype(jnp.bfloat16)
        slopes_ref[below, :] = silu.astype(jnp.bfloat16)
        hidden_ref[above, :] = (silu * up).astype(jnp.bfloat16)
        return 0

    lax.fori_loop(0, rows // STEP, some_rows, 0)
    parts_ref[:, : 2 * rank] = dot(in_ref[...], in_proj_ref[...])
    parts_ref[:, 2 * rank : 3 * rank] = dot(hidden_ref[...], hid_proj_ref[...])
    parts_ref[:, 3 * rank :] = dot(cot_ref[...], out_proj_ref[...])


def local_terms(pre, inputs, proj_in_x, proj_in_h, cotangent, proj_out_d):
    rows, hid = pre.shape[0] // 2, pre.shape[1]
    return pl.pallas_call(
        local_kernel,
        out_shape=(
            jax.ShapeDtypeStruct((2 * rows, hid), jnp.bfloat16),
            jax.ShapeDtypeStruct((rows, 4 * proj_out_d.shape[1]), jnp.float32),
        ),
        in_specs=[VMEM] * 6,
        out_specs=(VMEM, VMEM),
        scratch_shapes=[pltpu.VMEM((rows, hid), jnp.bfloat16)],
        compiler_params=pltpu.CompilerParams(vmem_limit_bytes=56 * 2**20),
        cost_estimate=pl.CostEstimate(flops=800 * rows * hid, bytes_accessed=8 * rows * hid, transcendentals=2 * rows * hid),
        name="local_terms",
    )(pre, inputs, proj_in_x, proj_in_h, cotangent, proj_out_d)


def gradient_kernel(
    yl_ref, blocks_hbm, weight_hbm, own_slopes, partner_slopes, proj_hbm, x_hbm, down_hbm, _,
    out_ref, cot, weight, slope, silu, proj_ref, x_ref, down_ref, total, rows_ref, sems,
):
    rank = down_hbm.shape[0]
    across, _, along, events, depth = blocks_hbm.shape
    cores, layers, _, hid = weight_hbm.shape
    layers = layers // CHUNKS
    span = cot.shape[1] // CHUNKS
    yl = yl_ref[0]
    own, partner = pl.ds(0, events), pl.ds(events, events)
    cot_moves = [
        (blocks_hbm.at[x, source, y], cot.at[rows, pl.ds((x * along + y) * depth, depth)])
        for x in range(across)
        for y in range(along)
        for source, rows in ((yl, own), (1 - yl, partner))
    ]
    weight_moves = [
        (weight_hbm.at[core, pl.ds(i * layers, layers)], weight.at[pl.ds(i * layers, layers), core])
        for i in range(CHUNKS)
        for core in range(cores)
    ]
    above, below = own, partner
    slope_moves = [(own_slopes.at[above], slope.at[own]), (partner_slopes.at[above], slope.at[partner])]
    slope_moves += [(own_slopes.at[below], silu.at[own]), (partner_slopes.at[below], silu.at[partner])]
    slope_moves += [(proj_hbm, proj_ref), (x_hbm, x_ref), (down_hbm, down_ref)]
    per_chunk = len(cot_moves) // CHUNKS
    copies = []
    for source, target in cot_moves + weight_moves + slope_moves:
        copies.append(pltpu.make_async_copy(source, target, sems.at[len(copies)]))
    of_cot, of_weight = copies[: len(cot_moves)], copies[len(cot_moves) :][: len(weight_moves)]
    of_slopes = copies[len(cot_moves) + len(weight_moves) :]
    of_chunk = [
        of_cot[i * per_chunk :][:per_chunk] + of_weight[i * cores :][:cores] for i in range(CHUNKS)
    ]
    for copy in sum(of_chunk, []) + of_slopes:
        copy.start()
    for i in range(CHUNKS):
        for copy in of_chunk[i]:
            copy.wait()
        rows_of_chunk = weight[pl.ds(i * layers, layers)].reshape(span, hid)
        term = dot(cot[:, pl.ds(i * span, span)], rows_of_chunk)
        if i == 0:
            total[...] = term
        elif i < CHUNKS - 1:
            total[...] += term
    grad = total[...] + term
    for copy in of_slopes:
        copy.wait()
    gate_sum = dot((grad * slope[...].astype(jnp.float32)).astype(jnp.bfloat16), proj_ref[...])
    up_sum = dot((grad * silu[...].astype(jnp.float32)).astype(jnp.bfloat16), proj_ref[...])
    lane = lax.broadcasted_iota(jnp.int32, gate_sum.shape, 1)
    both = jnp.where(lane < rank, gate_sum, up_sum)
    square = outer(x_ref[yl], both[:events]) + outer(x_ref[1 - yl], both[events:])
    rows_ref[:rank, :rank] = square[:rank, :rank]
    rows_ref[rank : 2 * rank, :rank] = square[rank:, rank:]
    rows_ref[2 * rank :, :rank] = down_ref[...]
    rows_ref[:, rank:] = jnp.zeros_like(rows_ref[:, rank:])
    members = out_ref.shape[0]
    each = rows_ref.shape[0] // members
    for i in range(each):
        row = rows_ref[pl.ds(i, members, stride=each), :]
        out_ref[:, :, i * rank : (i + 1) * rank] = row[:, None, :rank]


def gradient_blocks(yl, blocks, weight, own_slopes, partner_slopes, proj, proj_x, block_d, arrival, members):
    rank = block_d.shape[0]
    cores, layers, features, hid = weight.shape
    rows, depth = 2 * blocks.shape[3], cores * layers * features
    anywhere = pl.BlockSpec(memory_space=pl.ANY)
    return pl.pallas_call(
        gradient_kernel,
        out_shape=jax.ShapeDtypeStruct((members, 1, 3 * rank * rank // members), jnp.float32),
        in_specs=[pl.BlockSpec(memory_space=pltpu.SMEM)] + [anywhere] * 8,
        out_specs=VMEM,
        scratch_shapes=[
            pltpu.VMEM((rows, depth), jnp.bfloat16),
            pltpu.VMEM((layers, cores, features, hid), jnp.bfloat16),
            pltpu.VMEM((rows, hid), jnp.bfloat16),
            pltpu.VMEM((rows, hid), jnp.bfloat16),
            pltpu.VMEM(proj.shape, jnp.bfloat16),
            pltpu.VMEM(proj_x.shape, jnp.float32),
            pltpu.VMEM(block_d.shape, jnp.float32),
            pltpu.VMEM((rows, hid), jnp.float32),
            pltpu.VMEM((3 * rank, 2 * rank), jnp.float32),
            pltpu.SemaphoreType.DMA((blocks.shape[0] * 2 * blocks.shape[2] + CHUNKS * cores + 7,)),
        ],
        compiler_params=pltpu.CompilerParams(vmem_limit_bytes=56 * 2**20),
        cost_estimate=pl.CostEstimate(
            flops=2 * rows * depth * hid,
            bytes_accessed=weight.size * 2,
            transcendentals=0,
        ),
        name="gradient_blocks",
    )(yl, blocks, weight, own_slopes, partner_slopes, proj, proj_x, block_d, arrival)


def score_kernel(scale, member_ref, rows_ref, *refs):
    *query_refs, out_ref = refs
    copies, sessions, _ = out_ref.shape
    groups = len(query_refs)
    left = (rows_ref[:, 0] + rows_ref[:, 1]).reshape(sessions, -1)
    terms = []
    for _ in range(3):
        terms.append(left.astype(jnp.bfloat16).astype(jnp.float32))
        left = left - terms[-1]
    terms = jnp.concatenate(terms, axis=0).astype(jnp.bfloat16)
    for flip, query_ref in enumerate(query_refs):
        products = dot(terms, query_ref[...])
        scores = products[:sessions] + (products[sessions : 2 * sessions] + products[2 * sessions :])
        for i in range(0, copies, groups):
            out_ref[i + (member_ref[0] ^ flip)] = scores * scale


def score_blocks(member, rows, queries, copies, scale):
    return pl.pallas_call(
        functools.partial(score_kernel, scale),
        out_shape=jax.ShapeDtypeStruct((copies, rows.shape[0], queries[0].shape[1]), jnp.float32),
        in_specs=[pl.BlockSpec(memory_space=pltpu.SMEM)] + [VMEM] * (1 + len(queries)),
        out_specs=VMEM,
        name="score_blocks",
    )(member, rows, *queries)


def outer(a, b):
    return lax.dot_general(
        a, b, (((0,), (0,)), ((), ())), precision=HIGHEST, preferred_element_type=jnp.float32
    )


def give_all(block, axes):
    n = lax.axis_size(axes)
    return lax.all_to_all(jnp.broadcast_to(block[None], (n,) + block.shape), axes, 0, 0)


def on_device(
    inputs,
    cotangent,
    gate_pre,
    up_pre,
    down_weight,
    proj_in_x,
    proj_in_h,
    proj_out_ff,
    proj_out_d,
    queries,
    lengths,
):
    rows, width = cotangent.shape
    hid = gate_pre.shape[1]
    rank = proj_in_h.shape[1]
    own_yl = lax.axis_index("yl")
    tensor_size = lax.axis_size(TENSOR)

    weight = lax.all_gather(down_weight.T, ("c", "zh", "zl"), axis=0)
    weight = weight.reshape(lax.axis_size("c"), -1, *weight.shape[1:])

    per_half = cotangent.reshape(rows, -1, 2, 2 * down_weight.shape[1]).transpose(2, 0, 1, 3)
    per_half = per_half.reshape(2, 1, rows, width // 2)
    per_half = jnp.broadcast_to(per_half, (2, lax.axis_size("yh"), rows, width // 2))
    along_y = lax.all_to_all(per_half.reshape(-1, rows, width // 2), ("yl", "yh"), 0, 0)

    both_pre = jnp.concatenate([gate_pre, up_pre], axis=0)
    own_slopes, parts = local_terms(both_pre, inputs, proj_in_x, proj_in_h, cotangent, proj_out_d)

    along_y = jnp.broadcast_to(along_y[None], (lax.axis_size("x"),) + along_y.shape)
    along_y, own_slopes = lax.optimization_barrier((along_y, own_slopes))
    along_x = lax.all_to_all(along_y, "x", 0, 0).reshape(-1, 2, lax.axis_size("yh"), rows, width // 2)

    partner_slopes = lax.ppermute(own_slopes, "yl", SWAP)

    groups = lax.axis_size(QUERY_GROUP)
    member = lax.axis_index(QUERY_GROUP)
    quarters = queries.T.reshape(groups, -1, queries.shape[0])
    arrivals = []
    for flip in range(groups):
        piece = lax.dynamic_index_in_dim(quarters, member ^ flip, 0, keepdims=False)
        pairs = [(i, i ^ flip) for i in range(groups)]
        arrivals.append(lax.ppermute(piece, QUERY_GROUP, pairs) if flip else piece)

    yl = own_yl.reshape(1)

    some = rows // tensor_size
    parts, along_x = lax.optimization_barrier((parts, along_x))
    sums = lax.all_to_all(parts.reshape(tensor_size, some, 4 * rank), TENSOR, 0, 0).sum(axis=0)

    sums, arrivals[1], arrivals[2] = lax.optimization_barrier((sums, arrivals[1], arrivals[2]))
    first_event = lax.axis_index(DP) * rows + lax.axis_index(TENSOR) * some
    positions = first_event % LEN + jnp.arange(some, dtype=jnp.int32)
    live = (positions < lengths[first_event // LEN]).astype(jnp.float32)[:, None]
    sums_x, sums_h, sums_d = sums[:, : 2 * rank] * live, sums[:, 2 * rank : 3 * rank], sums[:, 3 * rank :]
    block_d = jnp.einsum("tr,ts->rs", sums_h, sums_d * live, precision=HIGHEST)
    proj_x = give_all(sums_x, ("yl",) + TENSOR).reshape(2, rows, 2 * rank)

    proj_x, arrivals[3] = lax.optimization_barrier((proj_x, arrivals[3]))

    members = tensor_size * groups
    blocks = gradient_blocks(
        yl, along_x, weight, own_slopes, partner_slopes, proj_out_ff, proj_x, block_d, arrivals[3], members
    )

    entries = lax.all_to_all(blocks, SHARE, 0, 0).sum(axis=0)
    entries = give_all(entries, ("zh", "zl"))
    entries = entries.reshape(-1, lax.axis_size("zl"), *entries.shape[1:])
    partial_scores = score_blocks(member.reshape(1), entries, arrivals, members, 1.0 / math.sqrt(LEN))
    return lax.all_to_all(partial_scores, SHARE, 0, 0).sum(axis=0)


def solution(mesh):
    fine = Mesh(mesh.devices.reshape(8, 2, 2, 2, 4, 2), DP + TENSOR)
    return jax.shard_map(
        on_device,
        mesh=fine,
        in_specs=(
            P(DP, TENSOR),
            P(DP, TENSOR),
            P(DP, TENSOR),
            P(DP, TENSOR),
            P(TENSOR, DP),
            P(TENSOR, None),
            P(TENSOR, None),
            P(TENSOR, None),
            P(TENSOR, None),
            P(DP, TENSOR),
            P(),
        ),
        out_specs=P(None, DP),
        check_vma=False,
    )
```

```python
import math

import jax
import jax.numpy as jnp
from jax import lax
from jax.experimental import pallas as pl
from jax.experimental.pallas import tpu as pltpu
from jax.sharding import Mesh
from jax.sharding import PartitionSpec as P

LEN = 2048
STEP = 32
CHUNKS = 4
DP = ("zh", "zl", "yl", "c")
TENSOR = ("x", "yh")
QUERY_GROUP = ("yl", "c")
SHARE = TENSOR + QUERY_GROUP
SWAP = [(0, 1), (1, 0)]
HIGHEST = lax.Precision.HIGHEST
VMEM = pl.BlockSpec(memory_space=pltpu.VMEM)


def dot(a, b):
    return jnp.dot(a, b, preferred_element_type=jnp.float32)


def local_kernel(pre_ref, in_ref, in_proj_ref, hid_proj_ref, cot_ref, out_proj_ref, slopes_ref, parts_ref, hidden_ref):
    rows = hidden_ref.shape[0]
    rank = out_proj_ref.shape[1]

    def some_rows(step, _):
        first = pl.multiple_of(step * STEP, STEP)
        above, below = pl.ds(first, STEP), pl.ds(rows + first, STEP)
        gate = pre_ref[above, :].astype(jnp.float32)
        up = pre_ref[below, :].astype(jnp.float32)
        sig = 1.0 / (1.0 + jnp.exp(-gate))
        silu = gate * sig
        slopes_ref[above, :] = (up * sig * (1.0 + gate * (1.0 - sig))).astype(jnp.bfloat16)
        slopes_ref[below, :] = silu.astype(jnp.bfloat16)
        hidden_ref[above, :] = (silu * up).astype(jnp.bfloat16)
        return 0

    lax.fori_loop(0, rows // STEP, some_rows, 0)
    parts_ref[:, : 2 * rank] = dot(in_ref[...], in_proj_ref[...])
    parts_ref[:, 2 * rank : 3 * rank] = dot(hidden_ref[...], hid_proj_ref[...])
    parts_ref[:, 3 * rank :] = dot(cot_ref[...], out_proj_ref[...])


def local_terms(pre, inputs, proj_in_x, proj_in_h, cotangent, proj_out_d):
    rows, hid = pre.shape[0] // 2, pre.shape[1]
    return pl.pallas_call(
        local_kernel,
        out_shape=(
            jax.ShapeDtypeStruct((2 * rows, hid), jnp.bfloat16),
            jax.ShapeDtypeStruct((rows, 4 * proj_out_d.shape[1]), jnp.float32),
        ),
        in_specs=[VMEM] * 6,
        out_specs=(VMEM, VMEM),
        scratch_shapes=[pltpu.VMEM((rows, hid), jnp.bfloat16)],
        compiler_params=pltpu.CompilerParams(vmem_limit_bytes=56 * 2**20),
        cost_estimate=pl.CostEstimate(flops=800 * rows * hid, bytes_accessed=8 * rows * hid, transcendentals=2 * rows * hid),
        name="local_terms",
    )(pre, inputs, proj_in_x, proj_in_h, cotangent, proj_out_d)


def gradient_kernel(
    yl_ref, blocks_hbm, weight_hbm, own_slopes, partner_slopes, proj_hbm, x_hbm, down_hbm, _,
    out_ref, cot, weight, slope, silu, proj_ref, x_ref, down_ref, total, rows_ref, sems,
):
    rank = down_hbm.shape[0]
    across, _, along, events, depth = blocks_hbm.shape
    cores, layers, _, hid = weight_hbm.shape
    layers = layers // CHUNKS
    span = cot.shape[1] // CHUNKS
    yl = yl_ref[0]
    own, partner = pl.ds(0, events), pl.ds(events, events)
    cot_moves = [
        (blocks_hbm.at[x, source, y], cot.at[rows, pl.ds((x * along + y) * depth, depth)])
        for x in range(across)
        for y in range(along)
        for source, rows in ((yl, own), (1 - yl, partner))
    ]
    weight_moves = [
        (weight_hbm.at[core, pl.ds(i * layers, layers)], weight.at[pl.ds(i * layers, layers), core])
        for i in range(CHUNKS)
        for core in range(cores)
    ]
    above, below = own, partner
    slope_moves = [(own_slopes.at[above], slope.at[own]), (partner_slopes.at[above], slope.at[partner])]
    slope_moves += [(own_slopes.at[below], silu.at[own]), (partner_slopes.at[below], silu.at[partner])]
    slope_moves += [(proj_hbm, proj_ref), (x_hbm, x_ref), (down_hbm, down_ref)]
    per_chunk = len(cot_moves) // CHUNKS
    copies = []
    for source, target in cot_moves + weight_moves + slope_moves:
        copies.append(pltpu.make_async_copy(source, target, sems.at[len(copies)]))
    of_cot, of_weight = copies[: len(cot_moves)], copies[len(cot_moves) :][: len(weight_moves)]
    of_slopes = copies[len(cot_moves) + len(weight_moves) :]
    of_chunk = [
        of_cot[i * per_chunk :][:per_chunk] + of_weight[i * cores :][:cores] for i in range(CHUNKS)
    ]
    for copy in sum(of_chunk, []) + of_slopes:
        copy.start()
    for i in range(CHUNKS):
        for copy in of_chunk[i]:
            copy.wait()
        rows_of_chunk = weight[pl.ds(i * layers, layers)].reshape(span, hid)
        term = dot(cot[:, pl.ds(i * span, span)], rows_of_chunk)
        if i == 0:
            total[...] = term
        elif i < CHUNKS - 1:
            total[...] += term
    grad = total[...] + term
    for copy in of_slopes:
        copy.wait()
    gate_sum = dot((grad * slope[...].astype(jnp.float32)).astype(jnp.bfloat16), proj_ref[...])
    up_sum = dot((grad * silu[...].astype(jnp.float32)).astype(jnp.bfloat16), proj_ref[...])
    lane = lax.broadcasted_iota(jnp.int32, gate_sum.shape, 1)
    both = jnp.where(lane < rank, gate_sum, up_sum)
    square = outer(x_ref[yl], both[:events]) + outer(x_ref[1 - yl], both[events:])
    rows_ref[:rank, :rank] = square[:rank, :rank]
    rows_ref[rank : 2 * rank, :rank] = square[rank:, rank:]
    rows_ref[2 * rank :, :rank] = down_ref[...]
    rows_ref[:, rank:] = jnp.zeros_like(rows_ref[:, rank:])
    members = out_ref.shape[0]
    each = rows_ref.shape[0] // members
    for i in range(each):
        row = rows_ref[pl.ds(i, members, stride=each), :]
        out_ref[:, :, i * rank : (i + 1) * rank] = row[:, None, :rank]


def gradient_blocks(yl, blocks, weight, own_slopes, partner_slopes, proj, proj_x, block_d, arrival, members):
    rank = block_d.shape[0]
    cores, layers, features, hid = weight.shape
    rows, depth = 2 * blocks.shape[3], cores * layers * features
    anywhere = pl.BlockSpec(memory_space=pl.ANY)
    return pl.pallas_call(
        gradient_kernel,
        out_shape=jax.ShapeDtypeStruct((members, 1, 3 * rank * rank // members), jnp.float32),
        in_specs=[pl.BlockSpec(memory_space=pltpu.SMEM)] + [anywhere] * 8,
        out_specs=VMEM,
        scratch_shapes=[
            pltpu.VMEM((rows, depth), jnp.bfloat16),
            pltpu.VMEM((layers, cores, features, hid), jnp.bfloat16),
            pltpu.VMEM((rows, hid), jnp.bfloat16),
            pltpu.VMEM((rows, hid), jnp.bfloat16),
            pltpu.VMEM(proj.shape, jnp.bfloat16),
            pltpu.VMEM(proj_x.shape, jnp.float32),
            pltpu.VMEM(block_d.shape, jnp.float32),
            pltpu.VMEM((rows, hid), jnp.float32),
            pltpu.VMEM((3 * rank, 2 * rank), jnp.float32),
            pltpu.SemaphoreType.DMA((blocks.shape[0] * 2 * blocks.shape[2] + CHUNKS * cores + 7,)),
        ],
        compiler_params=pltpu.CompilerParams(vmem_limit_bytes=56 * 2**20),
        cost_estimate=pl.CostEstimate(
            flops=2 * rows * depth * hid,
            bytes_accessed=weight.size * 2,
            transcendentals=0,
        ),
        name="gradient_blocks",
    )(yl, blocks, weight, own_slopes, partner_slopes, proj, proj_x, block_d, arrival)


def outer(a, b):
    return lax.dot_general(
        a, b, (((0,), (0,)), ((), ())), precision=HIGHEST, preferred_element_type=jnp.float32
    )


def give_all(block, axes):
    n = lax.axis_size(axes)
    return lax.all_to_all(jnp.broadcast_to(block[None], (n,) + block.shape), axes, 0, 0)


def on_device(
    inputs,
    cotangent,
    gate_pre,
    up_pre,
    down_weight,
    proj_in_x,
    proj_in_h,
    proj_out_ff,
    proj_out_d,
    queries,
    lengths,
):
    rows, width = cotangent.shape
    hid = gate_pre.shape[1]
    rank = proj_in_h.shape[1]
    own_yl = lax.axis_index("yl")
    tensor_size = lax.axis_size(TENSOR)

    weight = lax.all_gather(down_weight.T, ("c", "zh", "zl"), axis=0)
    weight = weight.reshape(lax.axis_size("c"), -1, *weight.shape[1:])

    per_half = cotangent.reshape(rows, -1, 2, 2 * down_weight.shape[1]).transpose(2, 0, 1, 3)
    per_half = per_half.reshape(2, 1, rows, width // 2)
    per_half = jnp.broadcast_to(per_half, (2, lax.axis_size("yh"), rows, width // 2))
    along_y = lax.all_to_all(per_half.reshape(-1, rows, width // 2), ("yl", "yh"), 0, 0)

    both_pre = jnp.concatenate([gate_pre, up_pre], axis=0)
    own_slopes, parts = local_terms(both_pre, inputs, proj_in_x, proj_in_h, cotangent, proj_out_d)

    along_y = jnp.broadcast_to(along_y[None], (lax.axis_size("x"),) + along_y.shape)
    along_y, own_slopes = lax.optimization_barrier((along_y, own_slopes))
    along_x = lax.all_to_all(along_y, "x", 0, 0).reshape(-1, 2, lax.axis_size("yh"), rows, width // 2)

    partner_slopes = lax.ppermute(own_slopes, "yl", SWAP)

    groups = lax.axis_size(QUERY_GROUP)
    member = lax.axis_index(QUERY_GROUP)
    quarters = queries.T.reshape(groups, -1, queries.shape[0])
    arrivals = []
    for flip in range(groups):
        piece = lax.dynamic_index_in_dim(quarters, member ^ flip, 0, keepdims=False)
        pairs = [(i, i ^ flip) for i in range(groups)]
        arrivals.append(lax.ppermute(piece, QUERY_GROUP, pairs) if flip else piece)

    yl = own_yl.reshape(1)

    some = rows // tensor_size
    parts, along_x = lax.optimization_barrier((parts, along_x))
    sums = lax.all_to_all(parts.reshape(tensor_size, some, 4 * rank), TENSOR, 0, 0).sum(axis=0)

    sums, arrivals[1], arrivals[2] = lax.optimization_barrier((sums, arrivals[1], arrivals[2]))
    first_event = lax.axis_index(DP) * rows + lax.axis_index(TENSOR) * some
    positions = first_event % LEN + jnp.arange(some, dtype=jnp.int32)
    live = (positions < lengths[first_event // LEN]).astype(jnp.float32)[:, None]
    sums_x, sums_h, sums_d = sums[:, : 2 * rank] * live, sums[:, 2 * rank : 3 * rank], sums[:, 3 * rank :]
    block_d = jnp.einsum("tr,ts->rs", sums_h, sums_d * live, precision=HIGHEST)
    proj_x = give_all(sums_x, ("yl",) + TENSOR).reshape(2, rows, 2 * rank)

    proj_x, arrivals[3] = lax.optimization_barrier((proj_x, arrivals[3]))

    members = tensor_size * groups
    blocks = gradient_blocks(
        yl, along_x, weight, own_slopes, partner_slopes, proj_out_ff, proj_x, block_d, arrivals[3], members
    )

    entries = lax.all_to_all(blocks, SHARE, 0, 0).sum(axis=0)
    entries = give_all(entries, ("zh", "zl"))
    entries = entries.reshape(-1, lax.axis_size("zl"), *entries.shape[1:])
    for bit in (1, 2):
        arrivals = [jnp.where(member & bit, arrivals[i ^ bit], arrivals[i]) for i in range(groups)]
    ordered = jnp.concatenate([arrivals[i] for i in (0, 2, 1, 3)], axis=1)
    partial_scores = jnp.dot(entries.sum(axis=1)[:, 0], ordered.astype(jnp.float32), precision=HIGHEST) * (1.0 / math.sqrt(LEN))
    partial_scores = partial_scores.reshape(-1, groups, queries.shape[0]).transpose(1, 0, 2)[:, None]
    partial_scores = jnp.broadcast_to(partial_scores, (groups, tensor_size) + partial_scores.shape[2:])
    partial_scores = partial_scores.reshape(members, *partial_scores.shape[2:])
    return lax.all_to_all(partial_scores, ("c", "yl", "yh", "x"), 0, 0).sum(axis=0)


def solution(mesh):
    fine = Mesh(mesh.devices.reshape(8, 2, 2, 2, 4, 2), DP + TENSOR)
    return jax.shard_map(
        on_device,
        mesh=fine,
        in_specs=(
            P(DP, TENSOR),
            P(DP, TENSOR),
            P(DP, TENSOR),
            P(DP, TENSOR),
            P(TENSOR, DP),
            P(TENSOR, None),
            P(TENSOR, None),
            P(TENSOR, None),
            P(TENSOR, None),
            P(DP, TENSOR),
            P(),
        ),
        out_specs=P(None, DP),
        check_vma=False,
    )
```

```python
import math

import jax
import jax.numpy as jnp
from jax import lax
from jax.experimental import pallas as pl
from jax.experimental.pallas import tpu as pltpu
from jax.sharding import Mesh
from jax.sharding import PartitionSpec as P

LEN = 2048
STEP = 32
CHUNKS = 4
DP = ("zh", "zl", "yl", "c")
TENSOR = ("x", "yh")
QUERY_GROUP = ("yl", "c")
SHARE = ("c", "yl", "yh", "x")
SWAP = [(0, 1), (1, 0)]
HIGHEST = lax.Precision.HIGHEST
VMEM = pl.BlockSpec(memory_space=pltpu.VMEM)


def dot(a, b):
    return jnp.dot(a, b, preferred_element_type=jnp.float32)


def local_kernel(pre_ref, in_ref, in_proj_ref, hid_proj_ref, cot_ref, out_proj_ref, slopes_ref, parts_ref, hidden_ref):
    rows, hid = hidden_ref.shape
    rank = out_proj_ref.shape[1]
    slopes_ref[:, hid:] = jnp.zeros((2 * rows, slopes_ref.shape[1] - hid), jnp.bfloat16)

    def some_rows(step, _):
        first = pl.multiple_of(step * STEP, STEP)
        above, below = pl.ds(first, STEP), pl.ds(rows + first, STEP)
        gate = pre_ref[above, :].astype(jnp.float32)
        up = pre_ref[below, :].astype(jnp.float32)
        sig = 1.0 / (1.0 + jnp.exp(-gate))
        silu = gate * sig
        slopes_ref[above, :hid] = (up * sig * (1.0 + gate * (1.0 - sig))).astype(jnp.bfloat16)
        slopes_ref[below, :hid] = silu.astype(jnp.bfloat16)
        hidden_ref[above, :] = (silu * up).astype(jnp.bfloat16)
        return 0

    lax.fori_loop(0, rows // STEP, some_rows, 0)
    parts_ref[:, : 2 * rank] = dot(in_ref[...], in_proj_ref[...])
    parts_ref[:, 2 * rank : 3 * rank] = dot(hidden_ref[...], hid_proj_ref[...])
    parts_ref[:, 3 * rank :] = dot(cot_ref[...], out_proj_ref[...])


def local_terms(pre, inputs, proj_in_x, proj_in_h, cotangent, proj_out_d):
    rows, hid = pre.shape[0] // 2, pre.shape[1]
    return pl.pallas_call(
        local_kernel,
        out_shape=(
            jax.ShapeDtypeStruct((2 * rows, -(-hid // 128) * 128), jnp.bfloat16),
            jax.ShapeDtypeStruct((rows, 4 * proj_out_d.shape[1]), jnp.float32),
        ),
        in_specs=[VMEM] * 6,
        out_specs=(VMEM, VMEM),
        scratch_shapes=[pltpu.VMEM((rows, hid), jnp.bfloat16)],
        compiler_params=pltpu.CompilerParams(vmem_limit_bytes=56 * 2**20),
        cost_estimate=pl.CostEstimate(flops=800 * rows * hid, bytes_accessed=8 * rows * hid, transcendentals=2 * rows * hid),
        name="local_terms",
    )(pre, inputs, proj_in_x, proj_in_h, cotangent, proj_out_d)


def gradient_kernel(
    yl_ref, blocks_hbm, weight_hbm, own_slopes, partner_slopes, proj_hbm, x_hbm, down_hbm, _,
    out_ref, cot, weight, slope, silu, proj_ref, x_ref, down_ref, total, rows_ref, sems,
):
    rank = down_hbm.shape[0]
    across, _, along, events, depth = blocks_hbm.shape
    cores, layers, _, hid = weight_hbm.shape
    layers = layers // CHUNKS
    span = cot.shape[1] // CHUNKS
    yl = yl_ref[0]
    own, partner = pl.ds(0, events), pl.ds(events, events)
    cot_moves = [
        (blocks_hbm.at[x, source, y], cot.at[rows, pl.ds((x * along + y) * depth, depth)])
        for x in range(across)
        for y in range(along)
        for source, rows in ((yl, own), (1 - yl, partner))
    ]
    weight_moves = [
        (weight_hbm.at[core, pl.ds(i * layers, layers)], weight.at[pl.ds(i * layers, layers), core])
        for i in range(CHUNKS)
        for core in range(cores)
    ]
    above, below = own, partner
    slope_moves = [(own_slopes.at[above], slope.at[own]), (partner_slopes.at[above], slope.at[partner])]
    slope_moves += [(own_slopes.at[below], silu.at[own]), (partner_slopes.at[below], silu.at[partner])]
    slope_moves += [(proj_hbm, proj_ref), (x_hbm, x_ref), (down_hbm, down_ref)]
    per_chunk = len(cot_moves) // CHUNKS
    copies = []
    for source, target in cot_moves + weight_moves + slope_moves:
        copies.append(pltpu.make_async_copy(source, target, sems.at[len(copies)]))
    of_cot, of_weight = copies[: len(cot_moves)], copies[len(cot_moves) :][: len(weight_moves)]
    of_slopes = copies[len(cot_moves) + len(weight_moves) :]
    of_chunk = [
        of_cot[i * per_chunk :][:per_chunk] + of_weight[i * cores :][:cores] for i in range(CHUNKS)
    ]
    for copy in sum(of_chunk, []) + of_slopes:
        copy.start()
    for i in range(CHUNKS):
        for copy in of_chunk[i]:
            copy.wait()
        rows_of_chunk = weight[pl.ds(i * layers, layers)].reshape(span, hid)
        term = dot(cot[:, pl.ds(i * span, span)], rows_of_chunk)
        if i == 0:
            total[...] = term
        elif i < CHUNKS - 1:
            total[...] += term
    grad = total[...] + term
    for copy in of_slopes:
        copy.wait()
    gate_sum = dot((grad * slope[:, :hid].astype(jnp.float32)).astype(jnp.bfloat16), proj_ref[...])
    up_sum = dot((grad * silu[:, :hid].astype(jnp.float32)).astype(jnp.bfloat16), proj_ref[...])
    lane = lax.broadcasted_iota(jnp.int32, gate_sum.shape, 1)
    both = jnp.where(lane < rank, gate_sum, up_sum)
    square = outer(x_ref[yl], both[:events]) + outer(x_ref[1 - yl], both[events:])
    rows_ref[:rank, :rank] = square[:rank, :rank]
    rows_ref[rank : 2 * rank, :rank] = square[rank:, rank:]
    rows_ref[2 * rank :, :rank] = down_ref[...]
    rows_ref[:, rank:] = jnp.zeros_like(rows_ref[:, rank:])
    members = out_ref.shape[0]
    each = rows_ref.shape[0] // members
    for group in range(members // across):
        core, low, high = group // 4, group // 2 % 2, group % 2
        first = high * 4 + low * 2 + core
        for i in range(each):
            row = rows_ref[pl.ds(first * each + i, across, stride=members // across * each), :]
            out_ref[group * across : (group + 1) * across, :, i * rank : (i + 1) * rank] = row[:, None, :rank]


def gradient_blocks(yl, blocks, weight, own_slopes, partner_slopes, proj, proj_x, block_d, arrival, members):
    rank = block_d.shape[0]
    cores, layers, features, hid = weight.shape
    rows, depth = 2 * blocks.shape[3], cores * layers * features
    padded = own_slopes.shape[1]
    anywhere = pl.BlockSpec(memory_space=pl.ANY)
    return pl.pallas_call(
        gradient_kernel,
        out_shape=jax.ShapeDtypeStruct((members, 1, 3 * rank * rank // members), jnp.float32),
        in_specs=[pl.BlockSpec(memory_space=pltpu.SMEM)] + [anywhere] * 8,
        out_specs=VMEM,
        scratch_shapes=[
            pltpu.VMEM((rows, depth), jnp.bfloat16),
            pltpu.VMEM((layers, cores, features, hid), jnp.bfloat16),
            pltpu.VMEM((rows, padded), jnp.bfloat16),
            pltpu.VMEM((rows, padded), jnp.bfloat16),
            pltpu.VMEM(proj.shape, jnp.bfloat16),
            pltpu.VMEM(proj_x.shape, jnp.float32),
            pltpu.VMEM(block_d.shape, jnp.float32),
            pltpu.VMEM((rows, hid), jnp.float32),
            pltpu.VMEM((3 * rank, 2 * rank), jnp.float32),
            pltpu.SemaphoreType.DMA((blocks.shape[0] * 2 * blocks.shape[2] + CHUNKS * cores + 7,)),
        ],
        compiler_params=pltpu.CompilerParams(vmem_limit_bytes=56 * 2**20),
        cost_estimate=pl.CostEstimate(
            flops=2 * rows * depth * hid,
            bytes_accessed=weight.size * 2,
            transcendentals=0,
        ),
        name="gradient_blocks",
    )(yl, blocks, weight, own_slopes, partner_slopes, proj, proj_x, block_d, arrival)


def outer(a, b):
    return lax.dot_general(
        a, b, (((0,), (0,)), ((), ())), precision=HIGHEST, preferred_element_type=jnp.float32
    )


def give_all(block, axes):
    n = lax.axis_size(axes)
    return lax.all_to_all(jnp.broadcast_to(block[None], (n,) + block.shape), axes, 0, 0)


def on_device(
    inputs,
    cotangent,
    gate_pre,
    up_pre,
    down_weight,
    proj_in_x,
    proj_in_h,
    proj_out_ff,
    proj_out_d,
    queries,
    lengths,
):
    rows, width = cotangent.shape
    hid = gate_pre.shape[1]
    rank = proj_in_h.shape[1]
    own_yl = lax.axis_index("yl")
    tensor_size = lax.axis_size(TENSOR)

    weight = lax.all_gather(down_weight.T, ("c", "zh", "zl"), axis=0)
    weight = weight.reshape(lax.axis_size("c"), -1, *weight.shape[1:])

    per_half = cotangent.reshape(rows, -1, 2, 2 * down_weight.shape[1]).transpose(2, 0, 1, 3)
    per_half = per_half.reshape(2, 1, rows, width // 2)
    per_half = jnp.broadcast_to(per_half, (2, lax.axis_size("yh"), rows, width // 2))
    along_y = lax.all_to_all(per_half.reshape(-1, rows, width // 2), ("yl", "yh"), 0, 0)

    both_pre = jnp.concatenate([gate_pre, up_pre], axis=0)
    own_slopes, parts = local_terms(both_pre, inputs, proj_in_x, proj_in_h, cotangent, proj_out_d)

    along_y = jnp.broadcast_to(along_y[None], (lax.axis_size("x"),) + along_y.shape)
    along_y, own_slopes = lax.optimization_barrier((along_y, own_slopes))
    along_x = lax.all_to_all(along_y, "x", 0, 0).reshape(-1, 2, lax.axis_size("yh"), rows, width // 2)

    partner_slopes = lax.ppermute(own_slopes, "yl", SWAP)

    groups = lax.axis_size(QUERY_GROUP)
    member = lax.axis_index(QUERY_GROUP)
    quarters = queries.T.reshape(groups, -1, queries.shape[0])
    arrivals = []
    for flip in range(groups):
        piece = lax.dynamic_index_in_dim(quarters, member ^ flip, 0, keepdims=False)
        pairs = [(i, i ^ flip) for i in range(groups)]
        arrivals.append(lax.ppermute(piece, QUERY_GROUP, pairs) if flip else piece)

    yl = own_yl.reshape(1)

    some = rows // tensor_size
    parts, along_x = lax.optimization_barrier((parts, along_x))
    sums = lax.all_to_all(parts.reshape(tensor_size, some, 4 * rank), TENSOR, 0, 0).sum(axis=0)

    sums, arrivals[1], arrivals[2] = lax.optimization_barrier((sums, arrivals[1], arrivals[2]))
    first_event = lax.axis_index(DP) * rows + lax.axis_index(TENSOR) * some
    positions = first_event % LEN + jnp.arange(some, dtype=jnp.int32)
    live = (positions < lengths[first_event // LEN]).astype(jnp.float32)[:, None]
    sums_x, sums_h, sums_d = sums[:, : 2 * rank] * live, sums[:, 2 * rank : 3 * rank], sums[:, 3 * rank :]
    block_d = jnp.einsum("tr,ts->rs", sums_h, sums_d * live, precision=HIGHEST)
    proj_x = give_all(sums_x, ("yl",) + TENSOR).reshape(2, rows, 2 * rank)

    proj_x, arrivals[3] = lax.optimization_barrier((proj_x, arrivals[3]))

    members = tensor_size * groups
    blocks = gradient_blocks(
        yl, along_x, weight, own_slopes, partner_slopes, proj_out_ff, proj_x, block_d, arrivals[3], members
    )

    entries = lax.all_to_all(blocks, SHARE, 0, 0).sum(axis=0)
    entries = give_all(entries, ("zh", "zl"))
    entries = entries.reshape(-1, lax.axis_size("zl"), *entries.shape[1:])
    for bit in (1, 2):
        arrivals = [jnp.where(member & bit, arrivals[i ^ bit], arrivals[i]) for i in range(groups)]
    ordered = jnp.concatenate([arrivals[i] for i in (0, 2, 1, 3)], axis=1)
    partial_scores = jnp.dot(entries.sum(axis=1)[:, 0], ordered.astype(jnp.float32), precision=HIGHEST) * (1.0 / math.sqrt(LEN))
    partial_scores = partial_scores.reshape(-1, groups, queries.shape[0]).transpose(1, 0, 2)[:, None]
    partial_scores = jnp.broadcast_to(partial_scores, (groups, tensor_size) + partial_scores.shape[2:])
    partial_scores = partial_scores.reshape(members, *partial_scores.shape[2:])
    return lax.all_to_all(partial_scores, SHARE, 0, 0).sum(axis=0)


def solution(mesh):
    fine = Mesh(mesh.devices.reshape(8, 2, 2, 2, 4, 2), DP + TENSOR)
    return jax.shard_map(
        on_device,
        mesh=fine,
        in_specs=(
            P(DP, TENSOR),
            P(DP, TENSOR),
            P(DP, TENSOR),
            P(DP, TENSOR),
            P(TENSOR, DP),
            P(TENSOR, None),
            P(TENSOR, None),
            P(TENSOR, None),
            P(TENSOR, None),
            P(DP, TENSOR),
            P(),
        ),
        out_specs=P(None, DP),
        check_vma=False,
    )
```

```python
import math

import jax
import jax.numpy as jnp
from jax import lax
from jax.experimental import pallas as pl
from jax.experimental.pallas import tpu as pltpu
from jax.sharding import Mesh
from jax.sharding import PartitionSpec as P

LEN = 2048
STEP = 32
CHUNKS = 4
DP = ("zh", "zl", "yl", "c")
TENSOR = ("x", "yh")
QUERY_GROUP = ("yl", "c")
SHARE = ("c", "yl", "yh", "x")
SWAP = [(0, 1), (1, 0)]
HIGHEST = lax.Precision.HIGHEST
VMEM = pl.BlockSpec(memory_space=pltpu.VMEM)


def dot(a, b):
    return jnp.dot(a, b, preferred_element_type=jnp.float32)


def local_kernel(pre_ref, in_ref, in_proj_ref, hid_proj_ref, cot_ref, out_proj_ref, slopes_ref, parts_ref, hidden_ref):
    rows, hid = hidden_ref.shape
    rank = out_proj_ref.shape[1]
    slopes_ref[:, hid:] = jnp.zeros((2 * rows, slopes_ref.shape[1] - hid), jnp.bfloat16)

    def some_rows(step, _):
        first = pl.multiple_of(step * STEP, STEP)
        above, below = pl.ds(first, STEP), pl.ds(rows + first, STEP)
        gate = pre_ref[above, :].astype(jnp.float32)
        up = pre_ref[below, :].astype(jnp.float32)
        sig = 1.0 / (1.0 + jnp.exp(-gate))
        silu = gate * sig
        slopes_ref[above, :hid] = (up * sig * (1.0 + gate * (1.0 - sig))).astype(jnp.bfloat16)
        slopes_ref[below, :hid] = silu.astype(jnp.bfloat16)
        hidden_ref[above, :] = (silu * up).astype(jnp.bfloat16)
        return 0

    lax.fori_loop(0, rows // STEP, some_rows, 0)
    parts_ref[:, : 2 * rank] = dot(in_ref[...], in_proj_ref[...])
    parts_ref[:, 2 * rank : 3 * rank] = dot(hidden_ref[...], hid_proj_ref[...])
    parts_ref[:, 3 * rank :] = dot(cot_ref[...], out_proj_ref[...])


def local_terms(pre, inputs, proj_in_x, proj_in_h, cotangent, proj_out_d):
    rows, hid = pre.shape[0] // 2, pre.shape[1]
    return pl.pallas_call(
        local_kernel,
        out_shape=(
            jax.ShapeDtypeStruct((2 * rows, -(-hid // 128) * 128), jnp.bfloat16),
            jax.ShapeDtypeStruct((rows, 4 * proj_out_d.shape[1]), jnp.float32),
        ),
        in_specs=[VMEM] * 6,
        out_specs=(VMEM, VMEM),
        scratch_shapes=[pltpu.VMEM((rows, hid), jnp.bfloat16)],
        compiler_params=pltpu.CompilerParams(vmem_limit_bytes=56 * 2**20),
        cost_estimate=pl.CostEstimate(flops=800 * rows * hid, bytes_accessed=8 * rows * hid, transcendentals=2 * rows * hid),
        name="local_terms",
    )(pre, inputs, proj_in_x, proj_in_h, cotangent, proj_out_d)


def gradient_kernel(
    yl_ref, blocks_hbm, weight_hbm, own_slopes, partner_slopes, proj_hbm, x_hbm, down_hbm, _,
    out_ref, cot, weight, slope, silu, proj_ref, x_ref, down_ref, total, rows_ref, sems,
):
    rank = down_hbm.shape[0]
    across, _, along, events, depth = blocks_hbm.shape
    cores, layers, _, hid = weight_hbm.shape
    layers = layers // CHUNKS
    span = cot.shape[1] // CHUNKS
    yl = yl_ref[0]
    own, partner = pl.ds(0, events), pl.ds(events, events)
    cot_moves = [
        (blocks_hbm.at[x, source, y], cot.at[rows, pl.ds((x * along + y) * depth, depth)])
        for x in range(across)
        for y in range(along)
        for source, rows in ((yl, own), (1 - yl, partner))
    ]
    weight_moves = [
        (weight_hbm.at[core, pl.ds(i * layers, layers)], weight.at[pl.ds(i * layers, layers), core])
        for i in range(CHUNKS)
        for core in range(cores)
    ]
    above, below = own, partner
    slope_moves = [(own_slopes.at[above], slope.at[own]), (partner_slopes.at[above], slope.at[partner])]
    slope_moves += [(own_slopes.at[below], silu.at[own]), (partner_slopes.at[below], silu.at[partner])]
    slope_moves += [(proj_hbm, proj_ref), (x_hbm, x_ref), (down_hbm, down_ref)]
    per_chunk = len(cot_moves) // CHUNKS
    copies = []
    for source, target in cot_moves + weight_moves + slope_moves:
        copies.append(pltpu.make_async_copy(source, target, sems.at[len(copies)]))
    of_cot, of_weight = copies[: len(cot_moves)], copies[len(cot_moves) :][: len(weight_moves)]
    of_slopes = copies[len(cot_moves) + len(weight_moves) :]
    of_chunk = [
        of_weight[i * cores :][:cores] + of_cot[i * per_chunk :][:per_chunk] for i in range(CHUNKS)
    ]
    for copy in sum(of_chunk, []) + of_slopes:
        copy.start()
    for i in range(CHUNKS):
        for copy in of_chunk[i]:
            copy.wait()
        rows_of_chunk = weight[pl.ds(i * layers, layers)].reshape(span, hid)
        term = dot(cot[:, pl.ds(i * span, span)], rows_of_chunk)
        if i == 0:
            total[...] = term
        elif i < CHUNKS - 1:
            total[...] += term
    grad = total[...] + term
    for copy in of_slopes:
        copy.wait()
    gate_sum = dot((grad * slope[:, :hid].astype(jnp.float32)).astype(jnp.bfloat16), proj_ref[...])
    up_sum = dot((grad * silu[:, :hid].astype(jnp.float32)).astype(jnp.bfloat16), proj_ref[...])
    lane = lax.broadcasted_iota(jnp.int32, gate_sum.shape, 1)
    both = jnp.where(lane < rank, gate_sum, up_sum)
    square = outer(x_ref[yl], both[:events]) + outer(x_ref[1 - yl], both[events:])
    rows_ref[:rank, :rank] = square[:rank, :rank]
    rows_ref[rank : 2 * rank, :rank] = square[rank:, rank:]
    rows_ref[2 * rank :, :rank] = down_ref[...]
    rows_ref[:, rank:] = jnp.zeros_like(rows_ref[:, rank:])
    members = out_ref.shape[0]
    each = rows_ref.shape[0] // members
    for group in range(members // across):
        core, low, high = group // 4, group // 2 % 2, group % 2
        first = high * 4 + low * 2 + core
        for i in range(each):
            row = rows_ref[pl.ds(first * each + i, across, stride=members // across * each), :]
            out_ref[group * across : (group + 1) * across, :, i * rank : (i + 1) * rank] = row[:, None, :rank]


def gradient_blocks(yl, blocks, weight, own_slopes, partner_slopes, proj, proj_x, block_d, arrival, members):
    rank = block_d.shape[0]
    cores, layers, features, hid = weight.shape
    rows, depth = 2 * blocks.shape[3], cores * layers * features
    padded = own_slopes.shape[1]
    anywhere = pl.BlockSpec(memory_space=pl.ANY)
    return pl.pallas_call(
        gradient_kernel,
        out_shape=jax.ShapeDtypeStruct((members, 1, 3 * rank * rank // members), jnp.float32),
        in_specs=[pl.BlockSpec(memory_space=pltpu.SMEM)] + [anywhere] * 8,
        out_specs=VMEM,
        scratch_shapes=[
            pltpu.VMEM((rows, depth), jnp.bfloat16),
            pltpu.VMEM((layers, cores, features, hid), jnp.bfloat16),
            pltpu.VMEM((rows, padded), jnp.bfloat16),
            pltpu.VMEM((rows, padded), jnp.bfloat16),
            pltpu.VMEM(proj.shape, jnp.bfloat16),
            pltpu.VMEM(proj_x.shape, jnp.float32),
            pltpu.VMEM(block_d.shape, jnp.float32),
            pltpu.VMEM((rows, hid), jnp.float32),
            pltpu.VMEM((3 * rank, 2 * rank), jnp.float32),
            pltpu.SemaphoreType.DMA((blocks.shape[0] * 2 * blocks.shape[2] + CHUNKS * cores + 7,)),
        ],
        compiler_params=pltpu.CompilerParams(vmem_limit_bytes=56 * 2**20),
        cost_estimate=pl.CostEstimate(
            flops=2 * rows * depth * hid,
            bytes_accessed=weight.size * 2,
            transcendentals=0,
        ),
        name="gradient_blocks",
    )(yl, blocks, weight, own_slopes, partner_slopes, proj, proj_x, block_d, arrival)


def outer(a, b):
    return lax.dot_general(
        a, b, (((0,), (0,)), ((), ())), precision=HIGHEST, preferred_element_type=jnp.float32
    )


def give_all(block, axes):
    n = lax.axis_size(axes)
    return lax.all_to_all(jnp.broadcast_to(block[None], (n,) + block.shape), axes, 0, 0)


def on_device(
    inputs,
    cotangent,
    gate_pre,
    up_pre,
    down_weight,
    proj_in_x,
    proj_in_h,
    proj_out_ff,
    proj_out_d,
    queries,
    lengths,
):
    rows, width = cotangent.shape
    hid = gate_pre.shape[1]
    rank = proj_in_h.shape[1]
    own_yl = lax.axis_index("yl")
    tensor_size = lax.axis_size(TENSOR)

    weight = lax.all_gather(down_weight.T, ("c", "zh", "zl"), axis=0)
    weight = weight.reshape(lax.axis_size("c"), -1, *weight.shape[1:])

    per_half = cotangent.reshape(rows, -1, 2, 2 * down_weight.shape[1]).transpose(2, 0, 1, 3)
    per_half = per_half.reshape(2, 1, rows, width // 2)
    per_half = jnp.broadcast_to(per_half, (2, lax.axis_size("yh"), rows, width // 2))
    along_y = lax.all_to_all(per_half.reshape(-1, rows, width // 2), ("yl", "yh"), 0, 0)

    both_pre = jnp.concatenate([gate_pre, up_pre], axis=0)
    own_slopes, parts = local_terms(both_pre, inputs, proj_in_x, proj_in_h, cotangent, proj_out_d)

    along_y = jnp.broadcast_to(along_y[None], (lax.axis_size("x"),) + along_y.shape)
    along_y, own_slopes = lax.optimization_barrier((along_y, own_slopes))
    along_x = lax.all_to_all(along_y, "x", 0, 0).reshape(-1, 2, lax.axis_size("yh"), rows, width // 2)

    partner_slopes = lax.ppermute(own_slopes, "yl", SWAP)

    groups = lax.axis_size(QUERY_GROUP)
    member = lax.axis_index(QUERY_GROUP)
    quarters = queries.T.reshape(groups, -1, queries.shape[0])
    arrivals = []
    for flip in range(groups):
        piece = lax.dynamic_index_in_dim(quarters, member ^ flip, 0, keepdims=False)
        pairs = [(i, i ^ flip) for i in range(groups)]
        arrivals.append(lax.ppermute(piece, QUERY_GROUP, pairs) if flip else piece)

    yl = own_yl.reshape(1)

    some = rows // tensor_size
    parts, along_x = lax.optimization_barrier((parts, along_x))
    sums = lax.all_to_all(parts.reshape(tensor_size, some, 4 * rank), TENSOR, 0, 0).sum(axis=0)

    sums, arrivals[1], arrivals[2] = lax.optimization_barrier((sums, arrivals[1], arrivals[2]))
    first_event = lax.axis_index(DP) * rows + lax.axis_index(TENSOR) * some
    positions = first_event % LEN + jnp.arange(some, dtype=jnp.int32)
    live = (positions < lengths[first_event // LEN]).astype(jnp.float32)[:, None]
    sums_x, sums_h, sums_d = sums[:, : 2 * rank] * live, sums[:, 2 * rank : 3 * rank], sums[:, 3 * rank :]
    block_d = jnp.einsum("tr,ts->rs", sums_h, sums_d * live, precision=HIGHEST)
    proj_x = give_all(sums_x, ("yl",) + TENSOR).reshape(2, rows, 2 * rank)

    proj_x, arrivals[3] = lax.optimization_barrier((proj_x, arrivals[3]))

    members = tensor_size * groups
    blocks = gradient_blocks(
        yl, along_x, weight, own_slopes, partner_slopes, proj_out_ff, proj_x, block_d, arrivals[3], members
    )

    entries = lax.all_to_all(blocks, SHARE, 0, 0).sum(axis=0)
    entries = give_all(entries, ("zh", "zl"))
    entries = entries.reshape(-1, lax.axis_size("zl"), *entries.shape[1:])
    for bit in (1, 2):
        arrivals = [jnp.where(member & bit, arrivals[i ^ bit], arrivals[i]) for i in range(groups)]
    ordered = jnp.concatenate([arrivals[i] for i in (0, 2, 1, 3)], axis=1)
    partial_scores = jnp.dot(entries.sum(axis=1)[:, 0], ordered.astype(jnp.float32), precision=HIGHEST) * (1.0 / math.sqrt(LEN))
    partial_scores = partial_scores.reshape(-1, groups, queries.shape[0]).transpose(1, 0, 2)[:, None]
    partial_scores = jnp.broadcast_to(partial_scores, (groups, tensor_size) + partial_scores.shape[2:])
    partial_scores = partial_scores.reshape(members, *partial_scores.shape[2:])
    return lax.all_to_all(partial_scores, SHARE, 0, 0).sum(axis=0)


def solution(mesh):
    fine = Mesh(mesh.devices.reshape(8, 2, 2, 2, 4, 2), DP + TENSOR)
    return jax.shard_map(
        on_device,
        mesh=fine,
        in_specs=(
            P(DP, TENSOR),
            P(DP, TENSOR),
            P(DP, TENSOR),
            P(DP, TENSOR),
            P(TENSOR, DP),
            P(TENSOR, None),
            P(TENSOR, None),
            P(TENSOR, None),
            P(TENSOR, None),
            P(DP, TENSOR),
            P(),
        ),
        out_specs=P(None, DP),
        check_vma=False,
    )
```
